256 devices in a mesh: az: 16 (over y_hi, z), ax: 4 (over x), obs: 4 (over y_lo, core).
Axes of the slice: x: 4, y: 4 (y_hi: 2, y_lo: 2; y = y_hi * 2 + y_lo), z: 8, core: 2. Of those that a mesh axis runs over, the one named last changes fastest.
Arguments:
- thickness: bfloat16 [1024, 128, 512], P('az', 'ax'), may hold values from -6 to 6
- loading: bfloat16 [1024, 128, 512], P('az', 'ax'), may hold values from -6 to 6
- kept_modes: int32 [64], replicated, may hold values from 0 to 511
- cap_stations: int32 [8], replicated, may hold values from 64 to 128
- observer_ids: int32 [1024], replicated, may hold values from 0 to 2047
Outputs:
- pressure: float32 [1024, 256], P(('az', 'obs'), 'ax')
The draws below stay inside these ranges and needn't reach their ends.
All inputs are finite; a program needn't handle non-finite values.
Results may differ from the reference program's by a relative error of at most 0.0055.
Values may be sent and summed in bfloat16 or wider, within the bound.
No kernel may reach another device: no remote copies, remote signals or barrier semaphores. Data moves between devices by JAX's collectives and lax.ppermute only.
A program may use at most 128 MiB of HBM per device.

```python
import math
import jax
import jax.numpy as jnp
from jax import lax

NAZ = 1024
SAMPLES = 512
FREQS = 128
MODES = 64
CAPS = 8
NZ = 128
OBSERVERS = 1024


def place_ends(drawn, key, least, high):
    index_at = [jax.random.randint(jax.random.fold_in(key, axis), (), 0, length) for axis, length in enumerate(drawn.shape)]
    main_axis = drawn.shape.index(max(drawn.shape))
    neighbour = index_at[:main_axis] + [(index_at[main_axis] + 1) % drawn.shape[main_axis]] + index_at[main_axis + 1:]
    return drawn.at[tuple(index_at)].set(least).at[tuple(neighbour)].set(high)


def steps_of(rng, dims, shards, low, top_value):
    gain, own = 1.0, jax.random.fold_in(rng, 6)
    for dim, blocks in shards:
        draws = jnp.exp(jax.random.uniform(jax.random.fold_in(own, dim), (blocks,), jnp.float32, low / len(shards), top_value / len(shards)))
        gain = gain * jnp.repeat(draws, dims[dim] // blocks).reshape([-1 if axis == dim else 1 for axis in range(len(dims))])
    return gain


def bell_draw(own_key, dims, deviation, bound, split=(), held_as=jnp.bfloat16):
    array = jax.random.normal(own_key, dims, jnp.float32) * deviation
    if len(split) > 0:
        array = steps_of(own_key, dims, split, -0.22, 0.18) * array
    return jnp.clip(array, min=-bound, max=bound).astype(held_as)


def setup_inputs(seed: int = 0) -> dict:
    key_list = jax.random.split(jax.random.key(seed), 6)
    thickness = bell_draw(key_list[0], (NAZ, NZ, SAMPLES), 1.0, 6.0, ((0, 16), (1, 4)))
    loading = bell_draw(key_list[1], (NAZ, NZ, SAMPLES), 1.0, 6.0, ((0, 16), (1, 4)))
    kept_modes = place_ends(jax.random.randint(key_list[2], (MODES,), 0, NAZ // 2), jax.random.fold_in(key_list[2], 1), 0, (NAZ // 2) - 1).astype(jnp.int32)
    cap_stations = place_ends(jax.random.randint(key_list[3], (CAPS,), NZ // 2, NZ + 1), jax.random.fold_in(key_list[3], 1), NZ // 2, NZ).astype(jnp.int32)
    observer_ids = place_ends(jax.random.randint(key_list[4], (OBSERVERS,), 0, 2048), jax.random.fold_in(key_list[4], 1), 0, 2047).astype(jnp.int32)
    return {"thickness": thickness, "loading": loading, "kept_modes": kept_modes, "cap_stations": cap_stations, "observer_ids": observer_ids}


SPACING = 0.1
RADIUS = 1.0
ARC = 10.0
KMAX = 6.0

def time_table(samples, first_bin, bin_count):
    steps = jnp.arange(samples, dtype=jnp.int32)
    bins = first_bin + jnp.arange(bin_count, dtype=jnp.int32) + 1
    angle = 2.0 * jnp.pi / samples * (steps[:, None] * bins[None, :] % samples).astype(jnp.float32)
    window = 0.5 - 0.5 * jnp.cos(2.0 * jnp.pi / samples * steps.astype(jnp.float32))
    factor = 2.0 / math.sqrt(samples)
    basis = jnp.concatenate([window[:, None] * jnp.cos(angle), -window[:, None] * jnp.sin(angle)], axis=1) * factor
    return basis.astype(jnp.bfloat16)

def mode_tables(positions, modes, total_az):
    angle = 2.0 * jnp.pi / total_az * (positions[:, None] * modes[None, :] % total_az).astype(jnp.float32)
    factor = 1.0 / math.sqrt(total_az)
    return ((jnp.cos(angle) * factor).astype(jnp.bfloat16), (jnp.sin(angle) * factor).astype(jnp.bfloat16))

def combine(cosine_part, sine_part):
    return jnp.stack([cosine_part[:, :, 0] + sine_part[:, :, 1], cosine_part[:, :, 1] - sine_part[:, :, 0], cosine_part[:, :, 2] + sine_part[:, :, 3], cosine_part[:, :, 3] - sine_part[:, :, 2]], axis=2)

def cap_weight(panel_index, stations):
    closed = (panel_index[:, None] < stations[None, :]).astype(jnp.float32)
    return lax.optimization_barrier(jnp.sum(closed, axis=1)) / stations.shape[0]

def pressure_term(observer_ids, total_z, panel_index, weight, modal, modes, total_freqs):
    polar = (observer_ids // 64).astype(jnp.float32)
    azimuth_index = observer_ids % 64
    theta = (20.0 + polar * (140.0 / 31.0)) * (jnp.pi / 180.0)
    axial_obs = 0.5 * SPACING * total_z + ARC * jnp.cos(theta)
    radial = ARC * jnp.sin(theta)
    axial_panel = (panel_index.astype(jnp.float32) + 0.5) * SPACING
    distance = jnp.sqrt((axial_obs[:, None] - axial_panel[None, :]) ** 2 + radial[:, None] ** 2 + RADIUS * RADIUS)
    inverse = 1.0 / distance
    radial_ratio = (radial[:, None] * inverse)[:, :, None]
    scaled = (inverse * weight[None, :])[:, :, None]
    inverse_three = inverse[:, :, None]
    mode_angle = 2.0 * jnp.pi / 64.0 * (modes[None, :] * azimuth_index[:, None] % 64).astype(jnp.float32)
    mode_cos = jnp.cos(mode_angle)[:, :, None]
    mode_sin = jnp.sin(mode_angle)[:, :, None]
    mode_count = modes.shape[0]
    block_width = min(32, total_freqs)
    reals = []
    imags = []
    for block_start in range(0, total_freqs, block_width):
        block_data = modal[:, :, :, block_start:block_start + block_width].astype(jnp.float32)
        wave = KMAX * (jnp.arange(block_width, dtype=jnp.int32) + block_start + 1).astype(jnp.float32) / total_freqs
        phase = distance[:, :, None] * wave[None, None, :]
        green_re = jnp.cos(phase) * scaled
        green_im = -jnp.sin(phase) * scaled
        thick_re = -wave * green_im
        thick_im = wave * green_re
        load_re = radial_ratio * (green_re * inverse_three - wave * green_im)
        load_im = radial_ratio * (wave * green_re + green_im * inverse_three)
        kernel = jnp.concatenate([thick_re, thick_im, load_re, load_im], axis=1)
        q_re = block_data[:, :, 0]
        q_im = block_data[:, :, 1]
        l_re = block_data[:, :, 2]
        l_im = block_data[:, :, 3]
        column_re = jnp.concatenate([q_re, -q_im, l_re, -l_im], axis=1)
        column_im = jnp.concatenate([q_im, q_re, l_im, l_re], axis=1)
        source = jnp.concatenate([column_re, column_im], axis=0)
        sums = jnp.einsum('okf,nkf->onf', kernel, source, precision=lax.Precision.HIGHEST)
        sum_re = sums[:, :mode_count]
        sum_im = sums[:, mode_count:]
        reals.append(lax.optimization_barrier(jnp.sum(mode_cos * sum_re - mode_sin * sum_im, axis=1)))
        imags.append(lax.optimization_barrier(jnp.sum(mode_cos * sum_im + mode_sin * sum_re, axis=1)))
    return jnp.concatenate([jnp.concatenate(reals, axis=1), jnp.concatenate(imags, axis=1)], axis=1)

def reference(thickness, loading, kept_modes, cap_stations, observer_ids):
    basis = time_table(SAMPLES, 0, FREQS)

    def transform_field(field):
        flat = jnp.dot(field.reshape(NAZ * NZ, SAMPLES), basis, preferred_element_type=jnp.float32)
        return flat.reshape(NAZ, NZ, 2, FREQS)
    spectrum = jnp.concatenate([transform_field(thickness), transform_field(loading)], axis=2).astype(jnp.bfloat16)
    mode_cos, mode_sin = mode_tables(jnp.arange(NAZ, dtype=jnp.int32), kept_modes, NAZ)
    wide = spectrum.reshape(NAZ, NZ * 4 * FREQS)
    cosine_part = jnp.dot(mode_cos.T, wide, preferred_element_type=jnp.float32).reshape(MODES, NZ, 4, FREQS)
    sine_part = jnp.dot(mode_sin.T, wide, preferred_element_type=jnp.float32).reshape(MODES, NZ, 4, FREQS)
    modal = combine(cosine_part, sine_part).astype(jnp.bfloat16)
    panel_index = jnp.arange(NZ, dtype=jnp.int32)
    weight = cap_weight(panel_index, cap_stations)
    partial_value = pressure_term(observer_ids, NZ, panel_index, weight, modal, kept_modes, FREQS)
    return partial_value * (1.0 / math.sqrt(NZ * MODES))
```

```python
import math

import jax
import jax.numpy as jnp
import numpy as np
from jax import lax
from jax.experimental import pallas as pl
from jax.experimental.pallas import tpu as pltpu
from jax.sharding import PartitionSpec as P

FREQS = 128
MODES = 64
POLARS = 32
ARC_POINTS = 64

SPACING = 0.1
RADIUS = 1.0
ARC = 10.0
KMAX = 6.0


def even_odd_series():
    nodes = np.cos((np.arange(64) + 0.5) * np.pi / 64) * 0.5 + 0.5
    root = np.sqrt(nodes)
    fit = np.polynomial.chebyshev.Chebyshev.fit
    even = fit(nodes, np.cos(np.pi * root), 7, domain=[0, 1]).convert(kind=np.polynomial.Polynomial)
    odd = fit(nodes, np.sin(np.pi * root) / root, 6, domain=[0, 1]).convert(
        kind=np.polynomial.Polynomial
    )
    return (
        [float(c) * 4.0**i for i, c in enumerate(even.coef)],
        [2.0 * float(c) * 4.0**i for i, c in enumerate(odd.coef)],
    )


EVEN, ODD = even_odd_series()


def series(coefficients, square):
    total = jnp.full_like(square, coefficients[-1])
    for c in coefficients[-2::-1]:
        total = total * square + c
    return total


def cos_sin_turns(turns):
    part = turns - jnp.round(turns)
    square = part * part
    return series(EVEN, square), part * series(ODD, square)


def time_table(samples, bin_count):
    steps = np.arange(samples)
    bins = np.arange(bin_count) + 1
    angle = 2.0 * np.pi / samples * (steps[:, None] * bins[None, :] % samples)
    window = 0.5 - 0.5 * np.cos(2.0 * np.pi / samples * steps)
    basis = np.concatenate([window[:, None] * np.cos(angle), -window[:, None] * np.sin(angle)], 1)
    return (basis * (2.0 / math.sqrt(samples))).astype(np.float32).astype(jnp.bfloat16)


def pair_sums(rows):
    row = lax.broadcasted_iota(jnp.int32, (8, 128), 0)
    low4, low2, low1 = (row & 4) == 0, (row & 2) == 0, (row & 1) == 0
    four = [
        jnp.where(low4, rows[i], rows[i + 4])
        + pltpu.roll(jnp.where(low4, rows[i + 4], rows[i]), 4, 0)
        for i in range(4)
    ]
    two = [
        jnp.where(
            low2, four[i] + pltpu.roll(four[i], 6, 0), four[i + 2] + pltpu.roll(four[i + 2], 2, 0)
        )
        for i in range(2)
    ]
    return jnp.where(low1, two[0] + pltpu.roll(two[0], 7, 0), two[1] + pltpu.roll(two[1], 1, 0))


def far_field(
    az_rows,
    z_rows,
    az_count,
    obs_count,
    total_az,
    total_z,
    ids_ref,
    caps_ref,
    modes_ref,
    basis_ref,
    thick_ref,
    load_ref,
    out_ref,
    field,
    spectrum,
    wave,
    green,
    sems,
):
    chunks = sems.shape[1]
    step = az_rows * z_rows // chunks
    copies = []
    for chunk in range(chunks):
        for f, source in enumerate((thick_ref, load_ref)):
            rows = pl.ds(chunk * step, step)
            copy = pltpu.make_async_copy(source.at[rows], field.at[f, rows], sems.at[f, chunk])
            copy.start()
            copies.append((f, chunk, copy))
    az, ax, obs = lax.axis_index("az"), lax.axis_index("ax"), lax.axis_index("obs")

    modes = jnp.concatenate([modes_ref[...], modes_ref[...]], axis=1)
    row = lax.broadcasted_iota(jnp.int32, (128, 128), 0)
    column = lax.broadcasted_iota(jnp.int32, (128, 128), 1)
    quarter = 256 * ((row >> 6) + (column >> 6))
    arc_phase = ((row & 63) * modes & 63) * (1024 // ARC_POINTS) - quarter
    arc, _ = cos_sin_turns(arc_phase.astype(jnp.float32) * (1.0 / 1024))
    turn = ((row & 63) + az * az_rows) * modes & (total_az - 1)
    ring, _ = cos_sin_turns((turn * (1024 // total_az) - quarter).astype(jnp.float32) * (1.0 / 1024))
    ring = (ring * (1.0 / math.sqrt(total_az))).astype(jnp.bfloat16)
    arc_high = arc.astype(jnp.bfloat16)
    arc_low = (arc - arc_high.astype(jnp.float32)).astype(jnp.bfloat16)
    contract = (((1,), (1,)), ((), ()))
    modal = lax.dot_general(arc_high, ring, contract, preferred_element_type=jnp.float32)
    modal += lax.dot_general(arc_low, ring, contract, preferred_element_type=jnp.float32)
    modal = modal.astype(jnp.bfloat16)

    bins = (lax.broadcasted_iota(jnp.int32, (1, 128), 1) + 1).astype(jnp.float32)
    wavenumber = KMAX / FREQS * bins
    panel = lax.broadcasted_iota(jnp.int32, (z_rows, 128), 0) + ax * z_rows
    weight = jnp.zeros((z_rows, 128), jnp.float32)
    for c in range(caps_ref.shape[0]):
        weight += (panel < caps_ref[c]).astype(jnp.float32)
    weight *= 1.0 / (caps_ref.shape[0] * math.sqrt(total_z * MODES))
    axial_panel = (panel.astype(jnp.float32) + 0.5) * SPACING

    def polar_step(p, carry):
        index = jnp.full((8, 128), p, jnp.int32).astype(jnp.float32)
        cos_theta, sin_theta = cos_sin_turns((20.0 + index * (140.0 / 31.0)) * (1.0 / 360.0))
        axial = (0.5 * SPACING * total_z + ARC * cos_theta)[:1]
        radial = (ARC * sin_theta)[:1]
        offset = axial - axial_panel
        distance = jnp.sqrt(offset * offset + (radial * radial + RADIUS * RADIUS))
        inverse = 1.0 / distance
        ratio = radial * inverse
        scaled = inverse * weight
        cos_phase, sin_phase = cos_sin_turns(distance * (wavenumber * (0.5 / math.pi)))
        re = cos_phase * scaled
        im = -sin_phase * scaled
        wave_re = wavenumber * re
        wave_im = wavenumber * im
        green[p, 0] = -wave_im
        green[p, 1] = wave_re
        green[p, 2] = ratio * (re * inverse - wave_im)
        green[p, 3] = ratio * (wave_re + im * inverse)
        return carry

    lax.fori_loop(0, POLARS, polar_step, 0, unroll=2)

    for f, chunk, copy in copies:
        copy.wait()
        rows = pl.ds(chunk * step, step)
        value = jnp.dot(field[f, rows], basis_ref[...], preferred_element_type=jnp.float32)
        spectrum[2 * f, rows] = value[:, :FREQS]
        spectrum[2 * f + 1, rows] = value[:, FREQS:]

    def panel_step(z, carry):
        rows = pl.ds(z, az_rows, stride=z_rows)
        parts = [spectrum[c, rows] for c in range(4)]
        source = jnp.concatenate(
            [
                jnp.concatenate([parts[0], parts[2]], axis=1),
                jnp.concatenate([parts[1], parts[3]], axis=1),
            ],
            axis=0,
        ).astype(jnp.bfloat16)
        value = jnp.dot(modal, source, preferred_element_type=jnp.float32)
        there = pl.ds(z, ARC_POINTS, stride=z_rows)
        wave[0, there] = value[:64, :128]
        wave[1, there] = value[64:, :128]
        wave[2, there] = value[:64, 128:]
        wave[3, there] = value[64:, 128:]
        return carry

    lax.fori_loop(0, z_rows, panel_step, 0, unroll=4)

    lane = lax.broadcasted_iota(jnp.int32, (8, 128), 1)
    per_block = ids_ref.shape[0] // (az_count * obs_count)

    def observer_block(block, carry):
        tops = []
        for half in range(2):
            reals, imags = [], []
            for j in range(8):
                where = ids_ref[(block * obs_count + obs) * per_block + half * 8 + j]
                p, q = where >> 6, where & 63
                rows = pl.ds(pl.multiple_of(q * z_rows, z_rows), z_rows)
                k0, k1, k2, k3 = (green[p, c] for c in range(4))
                w0, w1, w2, w3 = (wave[c, rows] for c in range(4))
                re = (k0 * w0 - k1 * w1) + (k2 * w2 - k3 * w3)
                im = (k0 * w1 + k1 * w0) + (k2 * w3 + k3 * w2)
                reals.append(jnp.sum(re.reshape(z_rows // 8, 8, 128), axis=0))
                imags.append(jnp.sum(im.reshape(z_rows // 8, 8, 128), axis=0))
            tops.append((pair_sums(reals), pair_sums(imags)))
        pieces = []
        for part in range(2):
            first, second = tops[0][part], tops[1][part]
            pieces.append(jnp.where(lane < 64, first, pltpu.roll(second, 64, 1)))
            pieces.append(jnp.where(lane < 64, pltpu.roll(first, 64, 1), second))
        rows = pl.ds(pl.multiple_of(block * 32, 32), 32)
        out_ref[rows] = jnp.concatenate(pieces, axis=0).astype(jnp.bfloat16)
        return carry

    lax.fori_loop(0, az_count, observer_block, 0)


def shards(thickness, loading, kept_modes, cap_stations, observer_ids):
    az_rows, z_rows, samples = thickness.shape
    az_count = lax.axis_size("az")
    ax_count = lax.axis_size("ax")
    obs_count = lax.axis_size("obs")
    total_az = az_rows * az_count
    total_z = z_rows * ax_count
    basis = jnp.asarray(time_table(samples, FREQS))
    chunks = 4
    flat = (az_rows * z_rows, samples)

    def body(*refs):
        far_field(az_rows, z_rows, az_count, obs_count, total_az, total_z, *refs)

    smem = pl.BlockSpec(memory_space=pltpu.SMEM)
    vmem = pl.BlockSpec(memory_space=pltpu.VMEM)
    anywhere = pl.BlockSpec(memory_space=pl.ANY)
    partial_value = pl.pallas_call(
        body,
        out_shape=jax.ShapeDtypeStruct((az_count * ax_count * 8, 128), jnp.bfloat16),
        in_specs=[smem, smem, vmem, vmem, anywhere, anywhere],
        out_specs=vmem,
        scratch_shapes=[
            pltpu.VMEM((2, *flat), jnp.bfloat16),
            pltpu.VMEM((4, az_rows * z_rows, FREQS), jnp.float32),
            pltpu.VMEM((4, ARC_POINTS * z_rows, FREQS), jnp.float32),
            pltpu.VMEM((POLARS, 4, z_rows, FREQS), jnp.float32),
            pltpu.SemaphoreType.DMA((2, chunks)),
        ],
        compiler_params=pltpu.CompilerParams(vmem_limit_bytes=48 * 1024 * 1024),
        name="far_field",
    )(
        observer_ids,
        cap_stations,
        kept_modes.reshape(1, MODES),
        basis,
        thickness.reshape(flat),
        loading.reshape(flat),
    )
    pieces = partial_value.reshape(az_count * ax_count, 8, 128)
    arrived = lax.all_to_all(pieces, ("az", "ax"), split_axis=0, concat_axis=0, tiled=True)
    total = jnp.sum(arrived.astype(jnp.float32), axis=0)
    return jnp.concatenate([total[:, :64], total[:, 64:]], axis=0)


def solution(mesh):
    return jax.shard_map(
        shards,
        mesh=mesh,
        in_specs=(P("az", "ax", None), P("az", "ax", None), P(), P(), P()),
        out_specs=P(("az", "obs"), "ax"),
        check_vma=False,
    )
```

```python
import math

import jax
import jax.numpy as jnp
import numpy as np
from jax import lax
from jax.experimental import pallas as pl
from jax.experimental.pallas import tpu as pltpu
from jax.sharding import PartitionSpec as P

FREQS = 128
MODES = 64
POLARS = 32
ARC_POINTS = 64
STRIDE = 40

SPACING = 0.1
RADIUS = 1.0
ARC = 10.0
KMAX = 6.0


def even_odd_series():
    nodes = np.cos((np.arange(64) + 0.5) * np.pi / 64) * 0.5 + 0.5
    root = np.sqrt(nodes)
    fit = np.polynomial.chebyshev.Chebyshev.fit
    even = fit(nodes, np.cos(np.pi * root), 7, domain=[0, 1]).convert(kind=np.polynomial.Polynomial)
    odd = fit(nodes, np.sin(np.pi * root) / root, 6, domain=[0, 1]).convert(
        kind=np.polynomial.Polynomial
    )
    return (
        [float(c) * 4.0**i for i, c in enumerate(even.coef)],
        [2.0 * float(c) * 4.0**i for i, c in enumerate(odd.coef)],
    )


EVEN, ODD = even_odd_series()


def series(coefficients, square):
    total = jnp.full_like(square, coefficients[-1])
    for c in coefficients[-2::-1]:
        total = total * square + c
    return total


def cos_sin_turns(turns):
    part = turns - jnp.round(turns)
    square = part * part
    return series(EVEN, square), part * series(ODD, square)


def time_table(samples, bin_count):
    steps = np.arange(samples)
    bins = np.arange(bin_count) + 1
    angle = 2.0 * np.pi / samples * (steps[:, None] * bins[None, :] % samples)
    window = 0.5 - 0.5 * np.cos(2.0 * np.pi / samples * steps)
    basis = np.concatenate([window[:, None] * np.cos(angle), -window[:, None] * np.sin(angle)], 1)
    return (basis * (2.0 / math.sqrt(samples))).astype(np.float32).astype(jnp.bfloat16)


def far_field(
    az_rows,
    z_rows,
    az_count,
    obs_count,
    total_az,
    total_z,
    ids_from,
    caps_from,
    modes_from,
    basis_from,
    thick_from,
    load_from,
    out_ref,
    ids_ref,
    caps_ref,
    modes_ref,
    basis_ref,
    field,
    spectrum,
    wave,
    green,
    sums,
    sems,
):
    fetch = [
        pltpu.make_async_copy(source, target, sems.at[i])
        for i, (source, target) in enumerate(
            (
                (caps_from, caps_ref),
                (modes_from, modes_ref),
                (basis_from, basis_ref),
                (thick_from, field.at[0]),
                (load_from, field.at[1]),
                (ids_from, ids_ref),
            )
        )
    ]
    for copy in fetch:
        copy.start()
    az, ax, obs = lax.axis_index("az"), lax.axis_index("ax"), lax.axis_index("obs")

    fetch[0].wait()
    bins = (lax.broadcasted_iota(jnp.int32, (1, 128), 1) + 1).astype(jnp.float32)
    wavenumber = KMAX / FREQS * bins
    panel = lax.broadcasted_iota(jnp.int32, (z_rows, 128), 0) + ax * z_rows
    weight = jnp.zeros((z_rows, 128), jnp.float32)
    for c in range(caps_ref.shape[0]):
        weight += (panel < caps_ref[c]).astype(jnp.float32)
    weight *= 1.0 / (caps_ref.shape[0] * math.sqrt(total_z * MODES))
    axial_panel = (panel.astype(jnp.float32) + 0.5) * SPACING

    def polar_step(p, carry):
        index = jnp.full((8, 128), p, jnp.int32).astype(jnp.float32)
        cos_theta, sin_theta = cos_sin_turns((20.0 + index * (140.0 / 31.0)) * (1.0 / 360.0))
        axial = (0.5 * SPACING * total_z + ARC * cos_theta)[:1]
        radial = (ARC * sin_theta)[:1]
        offset = axial - axial_panel
        distance = jnp.sqrt(offset * offset + (radial * radial + RADIUS * RADIUS))
        inverse = 1.0 / distance
        ratio = radial * inverse
        scaled = inverse * weight
        cos_phase, sin_phase = cos_sin_turns(distance * (wavenumber * (0.5 / math.pi)))
        re = cos_phase * scaled
        im = -sin_phase * scaled
        wave_re = wavenumber * re
        wave_im = wavenumber * im
        green[p, 0] = -wave_im
        green[p, 1] = wave_re
        green[p, 2] = ratio * (re * inverse - wave_im)
        green[p, 3] = ratio * (wave_re + im * inverse)
        return carry

    lax.fori_loop(0, POLARS, polar_step, 0, unroll=2)

    fetch[1].wait()
    modes = jnp.concatenate([modes_ref[...], modes_ref[...]], axis=1)
    row = lax.broadcasted_iota(jnp.int32, (128, 128), 0)
    column = lax.broadcasted_iota(jnp.int32, (128, 128), 1)
    quarter = 256 * ((row >> 6) + (column >> 6))
    arc_phase = ((row & 63) * modes & 63) * (1024 // ARC_POINTS) - quarter
    arc, _ = cos_sin_turns(arc_phase.astype(jnp.float32) * (1.0 / 1024))
    turn = ((row & 63) + az * az_rows) * modes & (total_az - 1)
    ring, _ = cos_sin_turns((turn * (1024 // total_az) - quarter).astype(jnp.float32) * (1.0 / 1024))
    ring = (ring * (1.0 / math.sqrt(total_az))).astype(jnp.bfloat16)
    arc_high = arc.astype(jnp.bfloat16)
    arc_low = (arc - arc_high.astype(jnp.float32)).astype(jnp.bfloat16)
    contract = (((1,), (1,)), ((), ()))
    modal = lax.dot_general(arc_high, ring, contract, preferred_element_type=jnp.float32)
    modal += lax.dot_general(arc_low, ring, contract, preferred_element_type=jnp.float32)
    modal = modal.astype(jnp.bfloat16)

    fetch[2].wait()
    for f in range(2):
        fetch[3 + f].wait()
        value = jnp.dot(field[f], basis_ref[...], preferred_element_type=jnp.float32)
        for i in range(az_rows):
            here = value[i * z_rows : (i + 1) * z_rows]
            there = pl.ds(i * STRIDE, z_rows)
            spectrum[2 * f, there] = here[:, :FREQS]
            spectrum[2 * f + 1, there] = here[:, FREQS:]

    def panel_step(z, carry):
        rows = pl.ds(z, az_rows, stride=STRIDE)
        parts = [spectrum[c, rows] for c in range(4)]
        source = jnp.concatenate(
            [
                jnp.concatenate([parts[0], parts[2]], axis=1),
                jnp.concatenate([parts[1], parts[3]], axis=1),
            ],
            axis=0,
        ).astype(jnp.bfloat16)
        value = jnp.dot(modal, source, preferred_element_type=jnp.float32)
        there = pl.ds(z, ARC_POINTS, stride=STRIDE)
        wave[0, there] = value[:64, :128]
        wave[1, there] = value[64:, :128]
        wave[2, there] = value[:64, 128:]
        wave[3, there] = value[64:, 128:]
        return carry

    lax.fori_loop(0, z_rows, panel_step, 0, unroll=8)

    fetch[5].wait()
    lane = lax.broadcasted_iota(jnp.int32, (8, 128), 1)
    per_block = ids_ref.shape[0] // (az_count * obs_count)

    def observer_step(block, carry):
        for j in range(per_block):
            where = ids_ref[(block * obs_count + obs) * per_block + j]
            p, q = where >> 6, where & 63
            rows = pl.ds(pl.multiple_of(q * STRIDE, 8), z_rows)
            k0, k1, k2, k3 = (green[p, c] for c in range(4))
            w0, w1, w2, w3 = (wave[c, rows] for c in range(4))
            re = (k0 * w0 - k1 * w1) + (k2 * w2 - k3 * w3)
            im = (k0 * w1 + k1 * w0) + (k2 * w3 + k3 * w2)
            there = pl.ds(pl.multiple_of((block * per_block + j) * 8, 8), 8)
            sums[0, there] = jnp.sum(re.reshape(z_rows // 8, 8, 128), axis=0)
            sums[1, there] = jnp.sum(im.reshape(z_rows // 8, 8, 128), axis=0)
        return carry

    lax.fori_loop(0, az_count, observer_step, 0)

    def gather_step(block, carry):
        pieces = []
        for part in range(2):
            halves = []
            for half in range(2):
                first = (block * per_block + half * 8) * 8
                rows = [sums[part, pl.ds(first + i, 8, stride=8)] for i in range(8)]
                while len(rows) > 1:
                    rows = [x + y for x, y in zip(rows[::2], rows[1::2])]
                halves.append(rows[0])
            low, high = halves
            pieces.append(jnp.where(lane < 64, low, pltpu.roll(high, 64, 1)))
            pieces.append(jnp.where(lane < 64, pltpu.roll(low, 64, 1), high))
        rows = pl.ds(pl.multiple_of(block * 32, 32), 32)
        out_ref[rows] = jnp.concatenate(pieces, axis=0).astype(jnp.bfloat16)
        return carry

    lax.fori_loop(0, az_count, gather_step, 0, unroll=2)


def shards(thickness, loading, kept_modes, cap_stations, observer_ids):
    az_rows, z_rows, samples = thickness.shape
    az_count = lax.axis_size("az")
    ax_count = lax.axis_size("ax")
    obs_count = lax.axis_size("obs")
    total_az = az_rows * az_count
    total_z = z_rows * ax_count
    basis = jnp.asarray(time_table(samples, FREQS))
    flat = (az_rows * z_rows, samples)

    def body(*refs):
        far_field(az_rows, z_rows, az_count, obs_count, total_az, total_z, *refs)

    anywhere = pl.BlockSpec(memory_space=pl.ANY)
    partial_value = pl.pallas_call(
        body,
        out_shape=jax.ShapeDtypeStruct((az_count * ax_count * 8, 128), jnp.bfloat16),
        in_specs=[anywhere] * 6,
        out_specs=pl.BlockSpec(memory_space=pltpu.VMEM),
        scratch_shapes=[
            pltpu.SMEM(observer_ids.shape, jnp.int32),
            pltpu.SMEM(cap_stations.shape, jnp.int32),
            pltpu.VMEM((1, MODES), jnp.int32),
            pltpu.VMEM(basis.shape, jnp.bfloat16),
            pltpu.VMEM((2, *flat), jnp.bfloat16),
            pltpu.VMEM((4, az_rows * STRIDE, FREQS), jnp.float32),
            pltpu.VMEM((4, ARC_POINTS * STRIDE, FREQS), jnp.float32),
            pltpu.VMEM((POLARS, 4, z_rows, FREQS), jnp.float32),
            pltpu.VMEM((2, observer_ids.shape[0] // obs_count * 8, FREQS), jnp.float32),
            pltpu.SemaphoreType.DMA((6,)),
        ],
        compiler_params=pltpu.CompilerParams(vmem_limit_bytes=60 * 1024 * 1024),
        name="far_field",
    )(
        observer_ids,
        cap_stations,
        kept_modes.reshape(1, MODES),
        basis,
        thickness.reshape(flat),
        loading.reshape(flat),
    )
    pieces = partial_value.reshape(az_count * ax_count, 8, 128)
    arrived = lax.all_to_all(pieces, ("az", "ax"), split_axis=0, concat_axis=0, tiled=True)
    total = jnp.sum(arrived.astype(jnp.float32), axis=0)
    return jnp.concatenate([total[:, :64], total[:, 64:]], axis=0)


def solution(mesh):
    return jax.shard_map(
        shards,
        mesh=mesh,
        in_specs=(P("az", "ax", None), P("az", "ax", None), P(), P(), P()),
        out_specs=P(("az", "obs"), "ax"),
        check_vma=False,
    )
```

```python
import math

import jax
import jax.numpy as jnp
import numpy as np
from jax import lax
from jax.experimental import pallas as pl
from jax.experimental.pallas import tpu as pltpu
from jax.sharding import PartitionSpec as P

FREQS = 128
MODES = 64
POLARS = 32
ARC_POINTS = 64
STRIDE = 40

SPACING = 0.1
RADIUS = 1.0
ARC = 10.0
KMAX = 6.0


Y_ORDER = (1, 0)
Z_ORDER = (4, 5, 6, 7, 3, 2, 1, 0)
AX_ORDER = (2, 3, 1, 0)


def exchange_groups(az_count, ax_count, obs_count):
    z_count = az_count // 2
    groups = []
    for twist in range(obs_count // 2):
        for core in range(2):
            groups.append(
                [
                    ((y * z_count + z) * ax_count + ax) * obs_count + 2 * (twist ^ y) + core
                    for y in Y_ORDER
                    for z in Z_ORDER
                    for ax in AX_ORDER
                ]
            )
    return groups


def even_odd_series():
    nodes = np.cos((np.arange(64) + 0.5) * np.pi / 64) * 0.5 + 0.5
    root = np.sqrt(nodes)
    fit = np.polynomial.chebyshev.Chebyshev.fit
    even = fit(nodes, np.cos(np.pi * root), 7, domain=[0, 1]).convert(kind=np.polynomial.Polynomial)
    odd = fit(nodes, np.sin(np.pi * root) / root, 6, domain=[0, 1]).convert(
        kind=np.polynomial.Polynomial
    )
    return (
        [float(c) * 4.0**i for i, c in enumerate(even.coef)],
        [2.0 * float(c) * 4.0**i for i, c in enumerate(odd.coef)],
    )


EVEN, ODD = even_odd_series()


def series(coefficients, square):
    total = jnp.full_like(square, coefficients[-1])
    for c in coefficients[-2::-1]:
        total = total * square + c
    return total


def cos_sin_turns(turns):
    part = turns - jnp.round(turns)
    square = part * part
    return series(EVEN, square), part * series(ODD, square)


def time_table(samples, bin_count):
    steps = np.arange(samples)
    bins = np.arange(bin_count) + 1
    angle = 2.0 * np.pi / samples * (steps[:, None] * bins[None, :] % samples)
    window = 0.5 - 0.5 * np.cos(2.0 * np.pi / samples * steps)
    basis = np.concatenate([window[:, None] * np.cos(angle), -window[:, None] * np.sin(angle)], 1)
    return (basis * (2.0 / math.sqrt(samples))).astype(np.float32).astype(jnp.bfloat16)


def far_field(
    az_rows,
    z_rows,
    az_count,
    obs_count,
    total_az,
    total_z,
    ids_from,
    caps_from,
    modes_from,
    basis_from,
    thick_from,
    load_from,
    out_ref,
    ids_ref,
    caps_ref,
    modes_ref,
    basis_ref,
    field,
    spectrum,
    wave,
    green,
    sums,
    sems,
):
    fetch = [
        pltpu.make_async_copy(source, target, sems.at[i])
        for i, (source, target) in enumerate(
            (
                (caps_from, caps_ref),
                (modes_from, modes_ref),
                (basis_from, basis_ref),
                (thick_from, field.at[0]),
                (load_from, field.at[1]),
                (ids_from, ids_ref),
            )
        )
    ]
    for copy in fetch:
        copy.start()
    az, ax, obs = lax.axis_index("az"), lax.axis_index("ax"), lax.axis_index("obs")

    fetch[0].wait()
    bins = (lax.broadcasted_iota(jnp.int32, (1, 128), 1) + 1).astype(jnp.float32)
    wavenumber = KMAX / FREQS * bins
    panel = lax.broadcasted_iota(jnp.int32, (z_rows, 128), 0) + ax * z_rows
    weight = jnp.zeros((z_rows, 128), jnp.float32)
    for c in range(caps_ref.shape[0]):
        weight += (panel < caps_ref[c]).astype(jnp.float32)
    weight *= 1.0 / (caps_ref.shape[0] * math.sqrt(total_z * MODES))
    axial_panel = (panel.astype(jnp.float32) + 0.5) * SPACING

    def polar_step(p, carry):
        index = jnp.full((8, 128), p, jnp.int32).astype(jnp.float32)
        cos_theta, sin_theta = cos_sin_turns((20.0 + index * (140.0 / 31.0)) * (1.0 / 360.0))
        axial = (0.5 * SPACING * total_z + ARC * cos_theta)[:1]
        radial = (ARC * sin_theta)[:1]
        offset = axial - axial_panel
        distance = jnp.sqrt(offset * offset + (radial * radial + RADIUS * RADIUS))
        inverse = 1.0 / distance
        ratio = radial * inverse
        scaled = inverse * weight
        cos_phase, sin_phase = cos_sin_turns(distance * (wavenumber * (0.5 / math.pi)))
        re = cos_phase * scaled
        im = -sin_phase * scaled
        wave_re = wavenumber * re
        wave_im = wavenumber * im
        green[p, 0] = -wave_im
        green[p, 1] = wave_re
        green[p, 2] = ratio * (re * inverse - wave_im)
        green[p, 3] = ratio * (wave_re + im * inverse)
        return carry

    lax.fori_loop(0, POLARS, polar_step, 0, unroll=2)

    fetch[1].wait()
    modes = jnp.concatenate([modes_ref[...], modes_ref[...]], axis=1)
    row = lax.broadcasted_iota(jnp.int32, (128, 128), 0)
    column = lax.broadcasted_iota(jnp.int32, (128, 128), 1)
    quarter = 256 * ((row >> 6) + (column >> 6))
    arc_phase = ((row & 63) * modes & 63) * (1024 // ARC_POINTS) - quarter
    arc, _ = cos_sin_turns(arc_phase.astype(jnp.float32) * (1.0 / 1024))
    turn = ((row & 63) + az * az_rows) * modes & (total_az - 1)
    ring, _ = cos_sin_turns((turn * (1024 // total_az) - quarter).astype(jnp.float32) * (1.0 / 1024))
    ring = (ring * (1.0 / math.sqrt(total_az))).astype(jnp.bfloat16)
    arc_high = arc.astype(jnp.bfloat16)
    arc_low = (arc - arc_high.astype(jnp.float32)).astype(jnp.bfloat16)
    contract = (((1,), (1,)), ((), ()))
    modal = lax.dot_general(arc_high, ring, contract, preferred_element_type=jnp.float32)
    modal += lax.dot_general(arc_low, ring, contract, preferred_element_type=jnp.float32)
    modal = modal.astype(jnp.bfloat16)

    fetch[2].wait()
    for f in range(2):
        fetch[3 + f].wait()
        value = jnp.dot(field[f], basis_ref[...], preferred_element_type=jnp.float32)
        for i in range(az_rows):
            here = value[i * z_rows : (i + 1) * z_rows]
            there = pl.ds(i * STRIDE, z_rows)
            spectrum[2 * f, there] = here[:, :FREQS]
            spectrum[2 * f + 1, there] = here[:, FREQS:]

    def panel_step(z, carry):
        rows = pl.ds(z, az_rows, stride=STRIDE)
        parts = [spectrum[c, rows] for c in range(4)]
        source = jnp.concatenate(
            [
                jnp.concatenate([parts[0], parts[2]], axis=1),
                jnp.concatenate([parts[1], parts[3]], axis=1),
            ],
            axis=0,
        ).astype(jnp.bfloat16)
        value = jnp.dot(modal, source, preferred_element_type=jnp.float32)
        there = pl.ds(z, ARC_POINTS, stride=STRIDE)
        wave[0, there] = value[:64, :128]
        wave[1, there] = value[64:, :128]
        wave[2, there] = value[:64, 128:]
        wave[3, there] = value[64:, 128:]
        return carry

    lax.fori_loop(0, z_rows, panel_step, 0, unroll=8)

    fetch[5].wait()
    lane = lax.broadcasted_iota(jnp.int32, (8, 128), 1)
    per_block = ids_ref.shape[0] // (az_count * obs_count)
    z_count = az_count // 2
    twist = (obs >> 1) ^ (az // z_count)

    def observer_step(block, carry):
        y = 1 - block // z_count
        z = block % z_count
        z = jnp.where(z < z_count // 2, z + z_count // 2, z_count - 1 - z)
        there_obs = 2 * (twist ^ y) + (obs & 1)
        first_id = ((y * z_count + z) * obs_count + there_obs) * per_block
        for j in range(per_block):
            where = ids_ref[first_id + j]
            p, q = where >> 6, where & 63
            rows = pl.ds(pl.multiple_of(q * STRIDE, 8), z_rows)
            k0, k1, k2, k3 = (green[p, c] for c in range(4))
            w0, w1, w2, w3 = (wave[c, rows] for c in range(4))
            re = (k0 * w0 - k1 * w1) + (k2 * w2 - k3 * w3)
            im = (k0 * w1 + k1 * w0) + (k2 * w3 + k3 * w2)
            there = pl.ds(pl.multiple_of((block * per_block + j) * 8, 8), 8)
            sums[0, there] = jnp.sum(re.reshape(z_rows // 8, 8, 128), axis=0)
            sums[1, there] = jnp.sum(im.reshape(z_rows // 8, 8, 128), axis=0)
        return carry

    lax.fori_loop(0, az_count, observer_step, 0)

    def gather_step(block, carry):
        pieces = []
        for part in range(2):
            halves = []
            for half in range(2):
                first = (block * per_block + half * 8) * 8
                rows = [sums[part, pl.ds(first + i, 8, stride=8)] for i in range(8)]
                while len(rows) > 1:
                    rows = [x + y for x, y in zip(rows[::2], rows[1::2])]
                halves.append(rows[0])
            low, high = halves
            pieces.append(jnp.where(lane < 64, low, pltpu.roll(high, 64, 1)))
            pieces.append(jnp.where(lane < 64, pltpu.roll(low, 64, 1), high))
        rows = pl.ds(pl.multiple_of(block * 32, 32), 32)
        out_ref[rows] = jnp.concatenate([pieces[ax] for ax in AX_ORDER], axis=0).astype(
            jnp.bfloat16
        )
        return carry

    lax.fori_loop(0, az_count, gather_step, 0, unroll=2)


def shards(thickness, loading, kept_modes, cap_stations, observer_ids):
    az_rows, z_rows, samples = thickness.shape
    az_count = lax.axis_size("az")
    ax_count = lax.axis_size("ax")
    obs_count = lax.axis_size("obs")
    total_az = az_rows * az_count
    total_z = z_rows * ax_count
    basis = jnp.asarray(time_table(samples, FREQS))
    flat = (az_rows * z_rows, samples)

    def body(*refs):
        far_field(az_rows, z_rows, az_count, obs_count, total_az, total_z, *refs)

    anywhere = pl.BlockSpec(memory_space=pl.ANY)
    partial_value = pl.pallas_call(
        body,
        out_shape=jax.ShapeDtypeStruct((az_count * ax_count * 8, 128), jnp.bfloat16),
        in_specs=[anywhere] * 6,
        out_specs=pl.BlockSpec(memory_space=pltpu.VMEM),
        scratch_shapes=[
            pltpu.SMEM(observer_ids.shape, jnp.int32),
            pltpu.SMEM(cap_stations.shape, jnp.int32),
            pltpu.VMEM((1, MODES), jnp.int32),
            pltpu.VMEM(basis.shape, jnp.bfloat16),
            pltpu.VMEM((2, *flat), jnp.bfloat16),
            pltpu.VMEM((4, az_rows * STRIDE, FREQS), jnp.float32),
            pltpu.VMEM((4, ARC_POINTS * STRIDE, FREQS), jnp.float32),
            pltpu.VMEM((POLARS, 4, z_rows, FREQS), jnp.float32),
            pltpu.VMEM((2, observer_ids.shape[0] // obs_count * 8, FREQS), jnp.float32),
            pltpu.SemaphoreType.DMA((6,)),
        ],
        compiler_params=pltpu.CompilerParams(vmem_limit_bytes=60 * 1024 * 1024),
        name="far_field",
    )(
        observer_ids,
        cap_stations,
        kept_modes.reshape(1, MODES),
        basis,
        thickness.reshape(flat),
        loading.reshape(flat),
    )
    pieces = partial_value.reshape(az_count * ax_count, 8, 128)
    arrived = lax.all_to_all(
        pieces,
        ("az", "ax", "obs"),
        split_axis=0,
        concat_axis=0,
        axis_index_groups=exchange_groups(az_count, ax_count, obs_count),
        tiled=True,
    )
    total = jnp.sum(arrived.astype(jnp.float32), axis=0)
    return jnp.concatenate([total[:, :64], total[:, 64:]], axis=0)


def solution(mesh):
    return jax.shard_map(
        shards,
        mesh=mesh,
        in_specs=(P("az", "ax", None), P("az", "ax", None), P(), P(), P()),
        out_specs=P(("az", "obs"), "ax"),
        check_vma=False,
    )
```

```python
import math

import jax
import jax.numpy as jnp
import numpy as np
from jax import lax
from jax.experimental import pallas as pl
from jax.experimental.pallas import tpu as pltpu
from jax.sharding import PartitionSpec as P

FREQS = 128
MODES = 64
POLARS = 32
ARC_POINTS = 64
STRIDE = 40

SPACING = 0.1
RADIUS = 1.0
ARC = 10.0
KMAX = 6.0


Y_ORDER = (1, 0)
Z_ORDER = (4, 5, 6, 7, 3, 2, 1, 0)
AX_ORDER = (2, 3, 1, 0)


def exchange_groups(az_count, ax_count, obs_count):
    z_count = az_count // 2
    groups = []
    for twist in range(obs_count // 2):
        for core in range(2):
            groups.append(
                [
                    ((y * z_count + z) * ax_count + ax) * obs_count + 2 * (twist ^ y) + core
                    for y in Y_ORDER
                    for z in Z_ORDER
                    for ax in AX_ORDER
                ]
            )
    return groups


def even_odd_series():
    nodes = np.cos((np.arange(64) + 0.5) * np.pi / 64) * 0.5 + 0.5
    root = np.sqrt(nodes)
    fit = np.polynomial.chebyshev.Chebyshev.fit
    even = fit(nodes, np.cos(np.pi * root), 7, domain=[0, 1]).convert(kind=np.polynomial.Polynomial)
    odd = fit(nodes, np.sin(np.pi * root) / root, 6, domain=[0, 1]).convert(
        kind=np.polynomial.Polynomial
    )
    return (
        [float(c) * 4.0**i for i, c in enumerate(even.coef)],
        [2.0 * float(c) * 4.0**i for i, c in enumerate(odd.coef)],
    )


EVEN, ODD = even_odd_series()


def series(coefficients, square):
    total = jnp.full_like(square, coefficients[-1])
    for c in coefficients[-2::-1]:
        total = total * square + c
    return total


def cos_sin_turns(turns):
    part = turns - jnp.round(turns)
    square = part * part
    return series(EVEN, square), part * series(ODD, square)


def time_table(samples, bin_count):
    steps = np.arange(samples)
    bins = np.arange(bin_count) + 1
    angle = 2.0 * np.pi / samples * (steps[:, None] * bins[None, :] % samples)
    window = 0.5 - 0.5 * np.cos(2.0 * np.pi / samples * steps)
    basis = np.concatenate([window[:, None] * np.cos(angle), -window[:, None] * np.sin(angle)], 1)
    return (basis * (2.0 / math.sqrt(samples))).astype(np.float32).astype(jnp.bfloat16)


def far_field(
    az_rows,
    z_rows,
    az_count,
    obs_count,
    total_az,
    total_z,
    ids_from,
    caps_from,
    modes_from,
    basis_from,
    thick_from,
    load_from,
    out_ref,
    ids_ref,
    caps_ref,
    modes_ref,
    basis_ref,
    field,
    spectrum,
    wave,
    green,
    sums,
    sems,
):
    fetch = [
        pltpu.make_async_copy(source, target, sems.at[i])
        for i, (source, target) in enumerate(
            (
                (caps_from, caps_ref),
                (modes_from, modes_ref),
                (basis_from, basis_ref),
                (thick_from, field.at[0]),
                (load_from, field.at[1]),
                (ids_from, ids_ref),
            )
        )
    ]
    for copy in fetch:
        copy.start()
    az, ax, obs = lax.axis_index("az"), lax.axis_index("ax"), lax.axis_index("obs")

    fetch[0].wait()
    bins = (lax.broadcasted_iota(jnp.int32, (1, 128), 1) + 1).astype(jnp.float32)
    wavenumber = KMAX / FREQS * bins
    panel = lax.broadcasted_iota(jnp.int32, (z_rows, 128), 0) + ax * z_rows
    weight = jnp.zeros((z_rows, 128), jnp.float32)
    for c in range(caps_ref.shape[0]):
        weight += (panel < caps_ref[c]).astype(jnp.float32)
    weight *= 1.0 / (caps_ref.shape[0] * math.sqrt(total_z * MODES))
    axial_panel = (panel.astype(jnp.float32) + 0.5) * SPACING

    def polar_step(p):
        index = jnp.full((8, 128), p, jnp.int32).astype(jnp.float32)
        cos_theta, sin_theta = cos_sin_turns((20.0 + index * (140.0 / 31.0)) * (1.0 / 360.0))
        axial = (0.5 * SPACING * total_z + ARC * cos_theta)[:1]
        radial = (ARC * sin_theta)[:1]
        offset = axial - axial_panel
        distance = jnp.sqrt(offset * offset + (radial * radial + RADIUS * RADIUS))
        inverse = 1.0 / distance
        ratio = radial * inverse
        scaled = inverse * weight
        cos_phase, sin_phase = cos_sin_turns(distance * (wavenumber * (0.5 / math.pi)))
        re = cos_phase * scaled
        im = -sin_phase * scaled
        wave_re = wavenumber * re
        wave_im = wavenumber * im
        green[p, 0] = -wave_im
        green[p, 1] = wave_re
        green[p, 2] = ratio * (re * inverse - wave_im)
        green[p, 3] = ratio * (wave_re + im * inverse)

    for p in range(POLARS):
        polar_step(p)

    fetch[1].wait()
    modes = jnp.concatenate([modes_ref[...], modes_ref[...]], axis=1)
    row = lax.broadcasted_iota(jnp.int32, (128, 128), 0)
    column = lax.broadcasted_iota(jnp.int32, (128, 128), 1)
    quarter = 256 * ((row >> 6) + (column >> 6))
    arc_phase = ((row & 63) * modes & 63) * (1024 // ARC_POINTS) - quarter
    arc, _ = cos_sin_turns(arc_phase.astype(jnp.float32) * (1.0 / 1024))
    turn = ((row & 63) + az * az_rows) * modes & (total_az - 1)
    ring, _ = cos_sin_turns((turn * (1024 // total_az) - quarter).astype(jnp.float32) * (1.0 / 1024))
    ring = (ring * (1.0 / math.sqrt(total_az))).astype(jnp.bfloat16)
    arc_high = arc.astype(jnp.bfloat16)
    arc_low = (arc - arc_high.astype(jnp.float32)).astype(jnp.bfloat16)
    contract = (((1,), (1,)), ((), ()))
    modal = lax.dot_general(arc_high, ring, contract, preferred_element_type=jnp.float32)
    modal += lax.dot_general(arc_low, ring, contract, preferred_element_type=jnp.float32)
    modal = modal.astype(jnp.bfloat16)

    for copy in fetch[2:5]:
        copy.wait()
    for f in range(2):
        for first in range(0, az_rows, 8):
            value = jnp.dot(
                field[f, first * z_rows : (first + 8) * z_rows],
                basis_ref[...],
                preferred_element_type=jnp.float32,
            )
            for i in range(8):
                here = value[i * z_rows : (i + 1) * z_rows]
                there = pl.ds((first + i) * STRIDE, z_rows)
                spectrum[2 * f, there] = here[:, :FREQS]
                spectrum[2 * f + 1, there] = here[:, FREQS:]

    def panel_step(z, carry):
        rows = pl.ds(z, az_rows, stride=STRIDE)
        parts = [spectrum[c, rows] for c in range(4)]
        source = jnp.concatenate(
            [
                jnp.concatenate([parts[0], parts[2]], axis=1),
                jnp.concatenate([parts[1], parts[3]], axis=1),
            ],
            axis=0,
        ).astype(jnp.bfloat16)
        value = jnp.dot(modal, source, preferred_element_type=jnp.float32)
        there = pl.ds(z, ARC_POINTS, stride=STRIDE)
        wave[0, there] = value[:64, :128]
        wave[1, there] = value[64:, :128]
        wave[2, there] = value[:64, 128:]
        wave[3, there] = value[64:, 128:]
        return carry

    lax.fori_loop(0, z_rows, panel_step, 0, unroll=8)

    fetch[5].wait()
    lane = lax.broadcasted_iota(jnp.int32, (8, 128), 1)
    per_block = ids_ref.shape[0] // (az_count * obs_count)
    z_count = az_count // 2
    twist = (obs >> 1) ^ (az // z_count)

    def observer_step(block, carry):
        y = 1 - block // z_count
        z = block % z_count
        z = jnp.where(z < z_count // 2, z + z_count // 2, z_count - 1 - z)
        there_obs = 2 * (twist ^ y) + (obs & 1)
        first_id = ((y * z_count + z) * obs_count + there_obs) * per_block
        for j in range(per_block):
            where = ids_ref[first_id + j]
            p, q = where >> 6, where & 63
            rows = pl.ds(pl.multiple_of(q * STRIDE, 8), z_rows)
            k0, k1, k2, k3 = (green[p, c] for c in range(4))
            w0, w1, w2, w3 = (wave[c, rows] for c in range(4))
            re = (k0 * w0 - k1 * w1) + (k2 * w2 - k3 * w3)
            im = (k0 * w1 + k1 * w0) + (k2 * w3 + k3 * w2)
            there = pl.ds(pl.multiple_of((block * per_block + j) * 8, 8), 8)
            sums[0, there] = jnp.sum(re.reshape(z_rows // 8, 8, 128), axis=0)
            sums[1, there] = jnp.sum(im.reshape(z_rows // 8, 8, 128), axis=0)
        return carry

    lax.fori_loop(0, az_count, observer_step, 0, unroll=2)

    def gather_step(block, carry):
        pieces = []
        for part in range(2):
            halves = []
            for half in range(2):
                first = (block * per_block + half * 8) * 8
                rows = [sums[part, pl.ds(first + i, 8, stride=8)] for i in range(8)]
                while len(rows) > 1:
                    rows = [x + y for x, y in zip(rows[::2], rows[1::2])]
                halves.append(rows[0])
            low, high = halves
            pieces.append(jnp.where(lane < 64, low, pltpu.roll(high, 64, 1)))
            pieces.append(jnp.where(lane < 64, pltpu.roll(low, 64, 1), high))
        rows = pl.ds(pl.multiple_of(block * 32, 32), 32)
        out_ref[rows] = jnp.concatenate([pieces[ax] for ax in AX_ORDER], axis=0).astype(
            jnp.bfloat16
        )
        return carry

    lax.fori_loop(0, az_count, gather_step, 0, unroll=8)


def shards(thickness, loading, kept_modes, cap_stations, observer_ids):
    az_rows, z_rows, samples = thickness.shape
    az_count = lax.axis_size("az")
    ax_count = lax.axis_size("ax")
    obs_count = lax.axis_size("obs")
    total_az = az_rows * az_count
    total_z = z_rows * ax_count
    basis = jnp.asarray(time_table(samples, FREQS))
    flat = (az_rows * z_rows, samples)

    def body(*refs):
        far_field(az_rows, z_rows, az_count, obs_count, total_az, total_z, *refs)

    anywhere = pl.BlockSpec(memory_space=pl.ANY)
    partial_value = pl.pallas_call(
        body,
        out_shape=jax.ShapeDtypeStruct((az_count * ax_count * 8, 128), jnp.bfloat16),
        in_specs=[anywhere] * 6,
        out_specs=pl.BlockSpec(memory_space=pltpu.VMEM),
        scratch_shapes=[
            pltpu.SMEM(observer_ids.shape, jnp.int32),
            pltpu.SMEM(cap_stations.shape, jnp.int32),
            pltpu.VMEM((1, MODES), jnp.int32),
            pltpu.VMEM(basis.shape, jnp.bfloat16),
            pltpu.VMEM((2, *flat), jnp.bfloat16),
            pltpu.VMEM((4, az_rows * STRIDE, FREQS), jnp.float32),
            pltpu.VMEM((4, ARC_POINTS * STRIDE, FREQS), jnp.float32),
            pltpu.VMEM((POLARS, 4, z_rows, FREQS), jnp.float32),
            pltpu.VMEM((2, observer_ids.shape[0] // obs_count * 8, FREQS), jnp.float32),
            pltpu.SemaphoreType.DMA((6,)),
        ],
        compiler_params=pltpu.CompilerParams(vmem_limit_bytes=60 * 1024 * 1024),
        name="far_field",
    )(
        observer_ids,
        cap_stations,
        kept_modes.reshape(1, MODES),
        basis,
        thickness.reshape(flat),
        loading.reshape(flat),
    )
    pieces = partial_value.reshape(az_count * ax_count, 8, 128)
    arrived = lax.all_to_all(
        pieces,
        ("az", "ax", "obs"),
        split_axis=0,
        concat_axis=0,
        axis_index_groups=exchange_groups(az_count, ax_count, obs_count),
        tiled=True,
    )
    total = jnp.sum(arrived.astype(jnp.float32), axis=0)
    return jnp.concatenate([total[:, :64], total[:, 64:]], axis=0)


def solution(mesh):
    return jax.shard_map(
        shards,
        mesh=mesh,
        in_specs=(P("az", "ax", None), P("az", "ax", None), P(), P(), P()),
        out_specs=P(("az", "obs"), "ax"),
        check_vma=False,
    )
```

```python
import math

import jax
import jax.numpy as jnp
import numpy as np
from jax import lax
from jax.experimental import pallas as pl
from jax.experimental.pallas import tpu as pltpu
from jax.sharding import PartitionSpec as P

FREQS = 128
MODES = 64
POLARS = 32
ARC_POINTS = 64
STRIDE = 40

SPACING = 0.1
RADIUS = 1.0
ARC = 10.0
KMAX = 6.0


Y_ORDER = (1, 0)
Z_ORDER = (4, 5, 6, 7, 3, 2, 1, 0)
AX_ORDER = (2, 3, 1, 0)


def exchange_groups(az_count, ax_count, obs_count):
    z_count = az_count // 2
    groups = []
    for twist in range(obs_count // 2):
        for core in range(2):
            groups.append(
                [
                    ((y * z_count + z) * ax_count + ax) * obs_count + 2 * (twist ^ y) + core
                    for y in Y_ORDER
                    for z in Z_ORDER
                    for ax in AX_ORDER
                ]
            )
    return groups


def even_odd_series():
    nodes = np.cos((np.arange(64) + 0.5) * np.pi / 64) * 0.5 + 0.5
    root = np.sqrt(nodes)
    fit = np.polynomial.chebyshev.Chebyshev.fit
    even = fit(nodes, np.cos(np.pi * root), 7, domain=[0, 1]).convert(kind=np.polynomial.Polynomial)
    odd = fit(nodes, np.sin(np.pi * root) / root, 6, domain=[0, 1]).convert(
        kind=np.polynomial.Polynomial
    )
    return (
        [float(c) * 4.0**i for i, c in enumerate(even.coef)],
        [2.0 * float(c) * 4.0**i for i, c in enumerate(odd.coef)],
    )


EVEN, ODD = even_odd_series()


def series(coefficients, square):
    total = jnp.full_like(square, coefficients[-1])
    for c in coefficients[-2::-1]:
        total = total * square + c
    return total


def cos_sin_turns(turns):
    part = turns - jnp.round(turns)
    square = part * part
    return series(EVEN, square), part * series(ODD, square)


def time_table(samples, bin_count):
    steps = np.arange(samples)
    bins = np.arange(bin_count) + 1
    angle = 2.0 * np.pi / samples * (steps[:, None] * bins[None, :] % samples)
    window = 0.5 - 0.5 * np.cos(2.0 * np.pi / samples * steps)
    basis = np.concatenate([window[:, None] * np.cos(angle), -window[:, None] * np.sin(angle)], 1)
    return (basis * (2.0 / math.sqrt(samples))).astype(np.float32).astype(jnp.bfloat16)


def far_field(
    az_rows,
    z_rows,
    az_count,
    obs_count,
    total_az,
    total_z,
    ids_from,
    caps_from,
    modes_from,
    basis_from,
    thick_from,
    load_from,
    out_ref,
    ids_ref,
    caps_ref,
    modes_ref,
    basis_ref,
    field,
    spectrum,
    wave,
    green,
    sums,
    sems,
):
    fetch = [
        pltpu.make_async_copy(source, target, sems.at[i])
        for i, (source, target) in enumerate(
            (
                (caps_from, caps_ref),
                (modes_from, modes_ref),
                (basis_from, basis_ref),
                (thick_from, field.at[0]),
                (load_from, field.at[1]),
                (ids_from, ids_ref),
            )
        )
    ]
    for copy in fetch:
        copy.start()
    az, ax, obs = lax.axis_index("az"), lax.axis_index("ax"), lax.axis_index("obs")

    fetch[0].wait()
    bins = (lax.broadcasted_iota(jnp.int32, (1, 128), 1) + 1).astype(jnp.float32)
    wavenumber = KMAX / FREQS * bins
    panel = lax.broadcasted_iota(jnp.int32, (z_rows, 128), 0) + ax * z_rows
    weight = jnp.zeros((z_rows, 128), jnp.float32)
    for c in range(caps_ref.shape[0]):
        weight += (panel < caps_ref[c]).astype(jnp.float32)
    weight *= 1.0 / (caps_ref.shape[0] * math.sqrt(total_z * MODES))
    axial_panel = (panel.astype(jnp.float32) + 0.5) * SPACING

    def polar_step(p):
        index = jnp.full((8, 128), p, jnp.int32).astype(jnp.float32)
        cos_theta, sin_theta = cos_sin_turns((20.0 + index * (140.0 / 31.0)) * (1.0 / 360.0))
        axial = (0.5 * SPACING * total_z + ARC * cos_theta)[:1]
        radial = (ARC * sin_theta)[:1]
        offset = axial - axial_panel
        distance = jnp.sqrt(offset * offset + (radial * radial + RADIUS * RADIUS))
        inverse = 1.0 / distance
        ratio = radial * inverse
        scaled = inverse * weight
        cos_phase, sin_phase = cos_sin_turns(distance * (wavenumber * (0.5 / math.pi)))
        re = cos_phase * scaled
        im = -sin_phase * scaled
        wave_re = wavenumber * re
        wave_im = wavenumber * im
        green[p, 0] = -wave_im
        green[p, 1] = wave_re
        green[p, 2] = ratio * (re * inverse - wave_im)
        green[p, 3] = ratio * (wave_re + im * inverse)

    for p in range(POLARS):
        polar_step(p)

    fetch[1].wait()
    modes = jnp.concatenate([modes_ref[...], modes_ref[...]], axis=1)
    row = lax.broadcasted_iota(jnp.int32, (128, 128), 0)
    column = lax.broadcasted_iota(jnp.int32, (128, 128), 1)
    quarter = 256 * ((row >> 6) + (column >> 6))
    arc_phase = ((row & 63) * modes & 63) * (1024 // ARC_POINTS) - quarter
    arc, _ = cos_sin_turns(arc_phase.astype(jnp.float32) * (1.0 / 1024))
    turn = ((row & 63) + az * az_rows) * modes & (total_az - 1)
    ring, _ = cos_sin_turns((turn * (1024 // total_az) - quarter).astype(jnp.float32) * (1.0 / 1024))
    ring = (ring * (1.0 / math.sqrt(total_az))).astype(jnp.bfloat16)
    arc_high = arc.astype(jnp.bfloat16)
    arc_low = (arc - arc_high.astype(jnp.float32)).astype(jnp.bfloat16)
    contract = (((1,), (1,)), ((), ()))
    modal = lax.dot_general(arc_high, ring, contract, preferred_element_type=jnp.float32)
    modal += lax.dot_general(arc_low, ring, contract, preferred_element_type=jnp.float32)
    modal = modal.astype(jnp.bfloat16)

    for copy in fetch[2:5]:
        copy.wait()
    for f in range(2):
        for first in range(0, az_rows, 8):
            value = jnp.dot(
                field[f, first * z_rows : (first + 8) * z_rows],
                basis_ref[...],
                preferred_element_type=jnp.float32,
            )
            for i in range(8):
                here = value[i * z_rows : (i + 1) * z_rows]
                there = pl.ds((first + i) * STRIDE, z_rows)
                spectrum[2 * f, there] = here[:, :FREQS]
                spectrum[2 * f + 1, there] = here[:, FREQS:]

    def panel_step(z, carry):
        rows = pl.ds(z, az_rows, stride=STRIDE)
        parts = [spectrum[c, rows] for c in range(4)]
        source = jnp.concatenate(
            [
                jnp.concatenate([parts[0], parts[2]], axis=1),
                jnp.concatenate([parts[1], parts[3]], axis=1),
            ],
            axis=0,
        ).astype(jnp.bfloat16)
        value = jnp.dot(modal, source, preferred_element_type=jnp.float32)
        there = pl.ds(z, ARC_POINTS, stride=STRIDE)
        wave[0, there] = value[:64, :128]
        wave[1, there] = value[64:, :128]
        wave[2, there] = value[:64, 128:]
        wave[3, there] = value[64:, 128:]
        return carry

    lax.fori_loop(0, z_rows, panel_step, 0, unroll=8)

    fetch[5].wait()
    lane = lax.broadcasted_iota(jnp.int32, (8, 128), 1)
    per_block = ids_ref.shape[0] // (az_count * obs_count)
    z_count = az_count // 2
    twist = (obs >> 1) ^ (az // z_count)

    def observer_step(block, carry):
        y = 1 - block // z_count
        z = block % z_count
        z = jnp.where(z < z_count // 2, z + z_count // 2, z_count - 1 - z)
        there_obs = 2 * (twist ^ y) + (obs & 1)
        first_id = ((y * z_count + z) * obs_count + there_obs) * per_block
        for j in range(per_block):
            where = ids_ref[first_id + j]
            p, q = where >> 6, where & 63
            rows = pl.ds(pl.multiple_of(q * STRIDE, 8), z_rows)
            k0, k1, k2, k3 = (green[p, c] for c in range(4))
            w0, w1, w2, w3 = (wave[c, rows] for c in range(4))
            re = (k0 * w0 - k1 * w1) + (k2 * w2 - k3 * w3)
            im = (k0 * w1 + k1 * w0) + (k2 * w3 + k3 * w2)
            there = pl.ds(pl.multiple_of((block * per_block + j) * 8, 8), 8)
            sums[0, there] = jnp.sum(re.reshape(z_rows // 8, 8, 128), axis=0)
            sums[1, there] = jnp.sum(im.reshape(z_rows // 8, 8, 128), axis=0)
        return carry

    lax.fori_loop(0, az_count, observer_step, 0, unroll=4)

    def gather_step(block, carry):
        pieces = []
        for part in range(2):
            halves = []
            for half in range(2):
                first = (block * per_block + half * 8) * 8
                rows = [sums[part, pl.ds(first + i, 8, stride=8)] for i in range(8)]
                while len(rows) > 1:
                    rows = [x + y for x, y in zip(rows[::2], rows[1::2])]
                halves.append(rows[0])
            low, high = halves
            pieces.append(jnp.where(lane < 64, low, pltpu.roll(high, 64, 1)))
            pieces.append(jnp.where(lane < 64, pltpu.roll(low, 64, 1), high))
        rows = pl.ds(pl.multiple_of(block * 32, 32), 32)
        out_ref[rows] = jnp.concatenate([pieces[ax] for ax in AX_ORDER], axis=0).astype(
            jnp.bfloat16
        )
        return carry

    lax.fori_loop(0, az_count, gather_step, 0, unroll=8)


def shards(thickness, loading, kept_modes, cap_stations, observer_ids):
    az_rows, z_rows, samples = thickness.shape
    az_count = lax.axis_size("az")
    ax_count = lax.axis_size("ax")
    obs_count = lax.axis_size("obs")
    total_az = az_rows * az_count
    total_z = z_rows * ax_count
    basis = jnp.asarray(time_table(samples, FREQS))
    flat = (az_rows * z_rows, samples)

    def body(*refs):
        far_field(az_rows, z_rows, az_count, obs_count, total_az, total_z, *refs)

    anywhere = pl.BlockSpec(memory_space=pl.ANY)
    partial_value = pl.pallas_call(
        body,
        out_shape=pltpu.VMEM((az_count * ax_count * 8, 128), jnp.bfloat16),
        in_specs=[anywhere] * 6,
        out_specs=pl.BlockSpec(memory_space=pltpu.VMEM),
        scratch_shapes=[
            pltpu.SMEM(observer_ids.shape, jnp.int32),
            pltpu.SMEM(cap_stations.shape, jnp.int32),
            pltpu.VMEM((1, MODES), jnp.int32),
            pltpu.VMEM(basis.shape, jnp.bfloat16),
            pltpu.VMEM((2, *flat), jnp.bfloat16),
            pltpu.VMEM((4, az_rows * STRIDE, FREQS), jnp.float32),
            pltpu.VMEM((4, ARC_POINTS * STRIDE, FREQS), jnp.float32),
            pltpu.VMEM((POLARS, 4, z_rows, FREQS), jnp.float32),
            pltpu.VMEM((2, observer_ids.shape[0] // obs_count * 8, FREQS), jnp.float32),
            pltpu.SemaphoreType.DMA((6,)),
        ],
        compiler_params=pltpu.CompilerParams(vmem_limit_bytes=60 * 1024 * 1024),
        name="far_field",
    )(
        observer_ids,
        cap_stations,
        kept_modes.reshape(1, MODES),
        basis,
        thickness.reshape(flat),
        loading.reshape(flat),
    )
    pieces = partial_value.reshape(az_count * ax_count, 8, 128)
    arrived = lax.all_to_all(
        pieces,
        ("az", "ax", "obs"),
        split_axis=0,
        concat_axis=0,
        axis_index_groups=exchange_groups(az_count, ax_count, obs_count),
        tiled=True,
    )
    total = jnp.sum(arrived.astype(jnp.float32), axis=0)
    return jnp.concatenate([total[:, :64], total[:, 64:]], axis=0)


def solution(mesh):
    return jax.shard_map(
        shards,
        mesh=mesh,
        in_specs=(P("az", "ax", None), P("az", "ax", None), P(), P(), P()),
        out_specs=P(("az", "obs"), "ax"),
        check_vma=False,
    )
```

```python
import math

import jax
import jax.numpy as jnp
import numpy as np
from jax import lax
from jax.experimental import pallas as pl
from jax.experimental.pallas import tpu as pltpu
from jax.sharding import PartitionSpec as P

FREQS = 128
MODES = 64
POLARS = 32
ARC_POINTS = 64
EARLY = 24
STRIDE = 40

SPACING = 0.1
RADIUS = 1.0
ARC = 10.0
KMAX = 6.0


Y_ORDER = (1, 0)
Z_ORDER = (4, 5, 6, 7, 3, 2, 1, 0)
AX_ORDER = (2, 3, 1, 0)


def exchange_groups(az_count, ax_count, obs_count):
    z_count = az_count // 2
    groups = []
    for twist in range(obs_count // 2):
        for core in range(2):
            groups.append(
                [
                    ((y * z_count + z) * ax_count + ax) * obs_count + 2 * (twist ^ y) + core
                    for y in Y_ORDER
                    for z in Z_ORDER
                    for ax in AX_ORDER
                ]
            )
    return groups


def even_odd_series():
    nodes = np.cos((np.arange(64) + 0.5) * np.pi / 64) * 0.5 + 0.5
    root = np.sqrt(nodes)
    fit = np.polynomial.chebyshev.Chebyshev.fit
    even = fit(nodes, np.cos(np.pi * root), 7, domain=[0, 1]).convert(kind=np.polynomial.Polynomial)
    odd = fit(nodes, np.sin(np.pi * root) / root, 6, domain=[0, 1]).convert(
        kind=np.polynomial.Polynomial
    )
    return (
        [float(c) * 4.0**i for i, c in enumerate(even.coef)],
        [2.0 * float(c) * 4.0**i for i, c in enumerate(odd.coef)],
    )


EVEN, ODD = even_odd_series()


def series(coefficients, square):
    total = jnp.full_like(square, coefficients[-1])
    for c in coefficients[-2::-1]:
        total = total * square + c
    return total


def cos_sin_turns(turns):
    part = turns - jnp.round(turns)
    square = part * part
    return series(EVEN, square), part * series(ODD, square)


def time_table(samples, bin_count):
    steps = np.arange(samples)
    bins = np.arange(bin_count) + 1
    angle = 2.0 * np.pi / samples * (steps[:, None] * bins[None, :] % samples)
    window = 0.5 - 0.5 * np.cos(2.0 * np.pi / samples * steps)
    basis = np.concatenate([window[:, None] * np.cos(angle), -window[:, None] * np.sin(angle)], 1)
    return (basis * (2.0 / math.sqrt(samples))).astype(np.float32).astype(jnp.bfloat16)


def far_field(
    az_rows,
    z_rows,
    az_count,
    obs_count,
    total_az,
    total_z,
    ids_from,
    caps_from,
    modes_from,
    basis_from,
    thick_from,
    load_from,
    out_ref,
    ids_ref,
    caps_ref,
    modes_ref,
    basis_ref,
    field,
    spectrum,
    wave,
    green,
    sums,
    sems,
):
    fetch = [
        pltpu.make_async_copy(source, target, sems.at[i])
        for i, (source, target) in enumerate(
            (
                (caps_from, caps_ref),
                (modes_from, modes_ref),
                (basis_from, basis_ref),
                (thick_from, field.at[0]),
                (load_from, field.at[1]),
                (ids_from, ids_ref),
            )
        )
    ]
    for copy in fetch:
        copy.start()
    az, ax, obs = lax.axis_index("az"), lax.axis_index("ax"), lax.axis_index("obs")

    fetch[0].wait()
    bins = (lax.broadcasted_iota(jnp.int32, (1, 128), 1) + 1).astype(jnp.float32)
    wavenumber = KMAX / FREQS * bins
    panel = lax.broadcasted_iota(jnp.int32, (z_rows, 128), 0) + ax * z_rows
    weight = jnp.zeros((z_rows, 128), jnp.float32)
    for c in range(caps_ref.shape[0]):
        weight += (panel < caps_ref[c]).astype(jnp.float32)
    weight *= 1.0 / (caps_ref.shape[0] * math.sqrt(total_z * MODES))
    axial_panel = (panel.astype(jnp.float32) + 0.5) * SPACING

    def polar_step(p):
        index = jnp.full((8, 128), p, jnp.int32).astype(jnp.float32)
        cos_theta, sin_theta = cos_sin_turns((20.0 + index * (140.0 / 31.0)) * (1.0 / 360.0))
        axial = (0.5 * SPACING * total_z + ARC * cos_theta)[:1]
        radial = (ARC * sin_theta)[:1]
        offset = axial - axial_panel
        distance = jnp.sqrt(offset * offset + (radial * radial + RADIUS * RADIUS))
        inverse = 1.0 / distance
        ratio = radial * inverse
        scaled = inverse * weight
        cos_phase, sin_phase = cos_sin_turns(distance * (wavenumber * (0.5 / math.pi)))
        re = cos_phase * scaled
        im = -sin_phase * scaled
        wave_re = wavenumber * re
        wave_im = wavenumber * im
        green[p, 0] = -wave_im
        green[p, 1] = wave_re
        green[p, 2] = ratio * (re * inverse - wave_im)
        green[p, 3] = ratio * (wave_re + im * inverse)

    for p in range(EARLY):
        polar_step(p)

    fetch[1].wait()
    modes = jnp.concatenate([modes_ref[...], modes_ref[...]], axis=1)
    row = lax.broadcasted_iota(jnp.int32, (128, 128), 0)
    column = lax.broadcasted_iota(jnp.int32, (128, 128), 1)
    quarter = 256 * ((row >> 6) + (column >> 6))
    arc_phase = ((row & 63) * modes & 63) * (1024 // ARC_POINTS) - quarter
    arc, _ = cos_sin_turns(arc_phase.astype(jnp.float32) * (1.0 / 1024))
    turn = ((row & 63) + az * az_rows) * modes & (total_az - 1)
    ring, _ = cos_sin_turns((turn * (1024 // total_az) - quarter).astype(jnp.float32) * (1.0 / 1024))
    ring = (ring * (1.0 / math.sqrt(total_az))).astype(jnp.bfloat16)
    arc_high = arc.astype(jnp.bfloat16)
    arc_low = (arc - arc_high.astype(jnp.float32)).astype(jnp.bfloat16)
    contract = (((1,), (1,)), ((), ()))
    modal = lax.dot_general(arc_high, ring, contract, preferred_element_type=jnp.float32)
    modal += lax.dot_general(arc_low, ring, contract, preferred_element_type=jnp.float32)
    modal = modal.astype(jnp.bfloat16)

    fetch[2].wait()
    for f in range(2):
        fetch[3 + f].wait()
        if f == 0:
            for p in range(EARLY, POLARS):
                polar_step(p)
        for first in range(0, az_rows, 8):
            value = jnp.dot(
                field[f, first * z_rows : (first + 8) * z_rows],
                basis_ref[...],
                preferred_element_type=jnp.float32,
            )
            for i in range(8):
                here = value[i * z_rows : (i + 1) * z_rows]
                there = pl.ds((first + i) * STRIDE, z_rows)
                spectrum[2 * f, there] = here[:, :FREQS]
                spectrum[2 * f + 1, there] = here[:, FREQS:]

    def panel_step(z, carry):
        rows = pl.ds(z, az_rows, stride=STRIDE)
        parts = [spectrum[c, rows] for c in range(4)]
        source = jnp.concatenate(
            [
                jnp.concatenate([parts[0], parts[2]], axis=1),
                jnp.concatenate([parts[1], parts[3]], axis=1),
            ],
            axis=0,
        ).astype(jnp.bfloat16)
        value = jnp.dot(modal, source, preferred_element_type=jnp.float32)
        there = pl.ds(z, ARC_POINTS, stride=STRIDE)
        wave[0, there] = value[:64, :128]
        wave[1, there] = value[64:, :128]
        wave[2, there] = value[:64, 128:]
        wave[3, there] = value[64:, 128:]
        return carry

    lax.fori_loop(0, z_rows, panel_step, 0, unroll=8)

    fetch[5].wait()
    lane = lax.broadcasted_iota(jnp.int32, (8, 128), 1)
    per_block = ids_ref.shape[0] // (az_count * obs_count)
    z_count = az_count // 2
    twist = (obs >> 1) ^ (az // z_count)

    def observer_step(block, carry):
        y = 1 - block // z_count
        z = block % z_count
        z = jnp.where(z < z_count // 2, z + z_count // 2, z_count - 1 - z)
        there_obs = 2 * (twist ^ y) + (obs & 1)
        first_id = ((y * z_count + z) * obs_count + there_obs) * per_block
        for j in range(per_block):
            where = ids_ref[first_id + j]
            p, q = where >> 6, where & 63
            rows = pl.ds(pl.multiple_of(q * STRIDE, 8), z_rows)
            k0, k1, k2, k3 = (green[p, c] for c in range(4))
            w0, w1, w2, w3 = (wave[c, rows] for c in range(4))
            re = (k0 * w0 - k1 * w1) + (k2 * w2 - k3 * w3)
            im = (k0 * w1 + k1 * w0) + (k2 * w3 + k3 * w2)
            there = pl.ds(pl.multiple_of((block * per_block + j) * 8, 8), 8)
            sums[0, there] = jnp.sum(re.reshape(z_rows // 8, 8, 128), axis=0)
            sums[1, there] = jnp.sum(im.reshape(z_rows // 8, 8, 128), axis=0)
        return carry

    lax.fori_loop(0, az_count, observer_step, 0, unroll=4)

    def gather_step(block, carry):
        pieces = []
        for part in range(2):
            halves = []
            for half in range(2):
                first = (block * per_block + half * 8) * 8
                rows = [sums[part, pl.ds(first + i, 8, stride=8)] for i in range(8)]
                while len(rows) > 1:
                    rows = [x + y for x, y in zip(rows[::2], rows[1::2])]
                halves.append(rows[0])
            low, high = halves
            pieces.append(jnp.where(lane < 64, low, pltpu.roll(high, 64, 1)))
            pieces.append(jnp.where(lane < 64, pltpu.roll(low, 64, 1), high))
        rows = pl.ds(pl.multiple_of(block * 32, 32), 32)
        out_ref[rows] = jnp.concatenate([pieces[ax] for ax in AX_ORDER], axis=0).astype(
            jnp.bfloat16
        )
        return carry

    lax.fori_loop(0, az_count, gather_step, 0, unroll=8)


def shards(thickness, loading, kept_modes, cap_stations, observer_ids):
    az_rows, z_rows, samples = thickness.shape
    az_count = lax.axis_size("az")
    ax_count = lax.axis_size("ax")
    obs_count = lax.axis_size("obs")
    total_az = az_rows * az_count
    total_z = z_rows * ax_count
    basis = jnp.asarray(time_table(samples, FREQS))
    flat = (az_rows * z_rows, samples)

    def body(*refs):
        far_field(az_rows, z_rows, az_count, obs_count, total_az, total_z, *refs)

    anywhere = pl.BlockSpec(memory_space=pl.ANY)
    partial_value = pl.pallas_call(
        body,
        out_shape=pltpu.VMEM((az_count * ax_count * 8, 128), jnp.bfloat16),
        in_specs=[anywhere] * 6,
        out_specs=pl.BlockSpec(memory_space=pltpu.VMEM),
        scratch_shapes=[
            pltpu.SMEM(observer_ids.shape, jnp.int32),
            pltpu.SMEM(cap_stations.shape, jnp.int32),
            pltpu.VMEM((1, MODES), jnp.int32),
            pltpu.VMEM(basis.shape, jnp.bfloat16),
            pltpu.VMEM((2, *flat), jnp.bfloat16),
            pltpu.VMEM((4, az_rows * STRIDE, FREQS), jnp.float32),
            pltpu.VMEM((4, ARC_POINTS * STRIDE, FREQS), jnp.float32),
            pltpu.VMEM((POLARS, 4, z_rows, FREQS), jnp.float32),
            pltpu.VMEM((2, observer_ids.shape[0] // obs_count * 8, FREQS), jnp.float32),
            pltpu.SemaphoreType.DMA((6,)),
        ],
        compiler_params=pltpu.CompilerParams(vmem_limit_bytes=60 * 1024 * 1024),
        name="far_field",
    )(
        observer_ids,
        cap_stations,
        kept_modes.reshape(1, MODES),
        basis,
        thickness.reshape(flat),
        loading.reshape(flat),
    )
    pieces = partial_value.reshape(az_count * ax_count, 8, 128)
    arrived = lax.all_to_all(
        pieces,
        ("az", "ax", "obs"),
        split_axis=0,
        concat_axis=0,
        axis_index_groups=exchange_groups(az_count, ax_count, obs_count),
        tiled=True,
    )
    total = jnp.sum(arrived.astype(jnp.float32), axis=0)
    return jnp.concatenate([total[:, :64], total[:, 64:]], axis=0)


def solution(mesh):
    return jax.shard_map(
        shards,
        mesh=mesh,
        in_specs=(P("az", "ax", None), P("az", "ax", None), P(), P(), P()),
        out_specs=P(("az", "obs"), "ax"),
        check_vma=False,
    )
```

```python
import math

import jax
import jax.numpy as jnp
import numpy as np
from jax import lax
from jax.experimental import pallas as pl
from jax.experimental.pallas import tpu as pltpu
from jax.sharding import PartitionSpec as P

FREQS = 128
MODES = 64
POLARS = 32
ARC_POINTS = 64
EARLY = 24
STRIDE = 40

SPACING = 0.1
RADIUS = 1.0
ARC = 10.0
KMAX = 6.0


Y_ORDER = (1, 0)
Z_ORDER = (4, 5, 6, 7, 3, 2, 1, 0)
AX_ORDER = (2, 3, 1, 0)


def exchange_groups(az_count, ax_count, obs_count):
    z_count = az_count // 2
    groups = []
    for twist in range(obs_count // 2):
        for core in range(2):
            groups.append(
                [
                    ((y * z_count + z) * ax_count + ax) * obs_count + 2 * (twist ^ y) + core
                    for y in Y_ORDER
                    for z in Z_ORDER
                    for ax in AX_ORDER
                ]
            )
    return groups


def even_odd_series():
    nodes = np.cos((np.arange(64) + 0.5) * np.pi / 64) * 0.5 + 0.5
    root = np.sqrt(nodes)
    fit = np.polynomial.chebyshev.Chebyshev.fit
    even = fit(nodes, np.cos(np.pi * root), 7, domain=[0, 1]).convert(kind=np.polynomial.Polynomial)
    odd = fit(nodes, np.sin(np.pi * root) / root, 6, domain=[0, 1]).convert(
        kind=np.polynomial.Polynomial
    )
    return (
        [float(c) * 4.0**i for i, c in enumerate(even.coef)],
        [2.0 * float(c) * 4.0**i for i, c in enumerate(odd.coef)],
    )


EVEN, ODD = even_odd_series()


def series(coefficients, square):
    total = jnp.full_like(square, coefficients[-1])
    for c in coefficients[-2::-1]:
        total = total * square + c
    return total


def cos_sin_turns(turns):
    part = turns - jnp.round(turns)
    square = part * part
    return series(EVEN, square), part * series(ODD, square)


def time_table(samples, bin_count):
    steps = np.arange(samples)
    bins = np.arange(bin_count) + 1
    angle = 2.0 * np.pi / samples * (steps[:, None] * bins[None, :] % samples)
    window = 0.5 - 0.5 * np.cos(2.0 * np.pi / samples * steps)
    basis = np.concatenate([window[:, None] * np.cos(angle), -window[:, None] * np.sin(angle)], 1)
    return (basis * (2.0 / math.sqrt(samples))).astype(np.float32).astype(jnp.bfloat16)


def far_field(
    az_rows,
    z_rows,
    az_count,
    obs_count,
    total_az,
    total_z,
    ids_from,
    caps_from,
    modes_from,
    basis_from,
    thick_from,
    load_from,
    out_ref,
    ids_ref,
    caps_ref,
    modes_ref,
    basis_ref,
    field,
    spectrum,
    wave,
    green,
    sums,
    sems,
):
    fetch = [
        pltpu.make_async_copy(source, target, sems.at[i])
        for i, (source, target) in enumerate(
            (
                (caps_from, caps_ref),
                (modes_from, modes_ref),
                (basis_from, basis_ref),
                (thick_from, field.at[0]),
                (load_from, field.at[1]),
                (ids_from, ids_ref),
            )
        )
    ]
    for copy in fetch:
        copy.start()
    az, ax, obs = lax.axis_index("az"), lax.axis_index("ax"), lax.axis_index("obs")

    fetch[0].wait()
    bins = (lax.broadcasted_iota(jnp.int32, (1, 128), 1) + 1).astype(jnp.float32)
    wavenumber = KMAX / FREQS * bins
    panel = lax.broadcasted_iota(jnp.int32, (z_rows, 128), 0) + ax * z_rows
    weight = jnp.zeros((z_rows, 128), jnp.float32)
    for c in range(caps_ref.shape[0]):
        weight += (panel < caps_ref[c]).astype(jnp.float32)
    weight *= 1.0 / (caps_ref.shape[0] * math.sqrt(total_z * MODES))
    axial_panel = (panel.astype(jnp.float32) + 0.5) * SPACING

    def polar_step(p):
        index = jnp.full((8, 128), p, jnp.int32).astype(jnp.float32)
        cos_theta, sin_theta = cos_sin_turns((20.0 + index * (140.0 / 31.0)) * (1.0 / 360.0))
        axial = (0.5 * SPACING * total_z + ARC * cos_theta)[:1]
        radial = (ARC * sin_theta)[:1]
        offset = axial - axial_panel
        distance = jnp.sqrt(offset * offset + (radial * radial + RADIUS * RADIUS))
        inverse = 1.0 / distance
        ratio = radial * inverse
        scaled = inverse * weight
        cos_phase, sin_phase = cos_sin_turns(distance * (wavenumber * (0.5 / math.pi)))
        re = cos_phase * scaled
        im = -sin_phase * scaled
        wave_re = wavenumber * re
        wave_im = wavenumber * im
        green[p, 0] = -wave_im
        green[p, 1] = wave_re
        green[p, 2] = ratio * (re * inverse - wave_im)
        green[p, 3] = ratio * (wave_re + im * inverse)

    for p in range(EARLY):
        polar_step(p)

    fetch[1].wait()
    modes = jnp.concatenate([modes_ref[...], modes_ref[...]], axis=1)
    row = lax.broadcasted_iota(jnp.int32, (128, 128), 0)
    column = lax.broadcasted_iota(jnp.int32, (128, 128), 1)
    quarter = 256 * ((row >> 6) + (column >> 6))
    arc_phase = ((row & 63) * modes & 63) * (1024 // ARC_POINTS) - quarter
    arc, _ = cos_sin_turns(arc_phase.astype(jnp.float32) * (1.0 / 1024))
    turn = ((row & 63) + az * az_rows) * modes & (total_az - 1)
    ring, _ = cos_sin_turns((turn * (1024 // total_az) - quarter).astype(jnp.float32) * (1.0 / 1024))
    ring = (ring * (1.0 / math.sqrt(total_az))).astype(jnp.bfloat16)
    arc_high = arc.astype(jnp.bfloat16)
    arc_low = (arc - arc_high.astype(jnp.float32)).astype(jnp.bfloat16)
    contract = (((1,), (1,)), ((), ()))
    modal = lax.dot_general(arc_high, ring, contract, preferred_element_type=jnp.float32)
    modal += lax.dot_general(arc_low, ring, contract, preferred_element_type=jnp.float32)
    modal = modal.astype(jnp.bfloat16)

    fetch[2].wait()
    for f in range(2):
        fetch[3 + f].wait()
        if f == 0:
            for p in range(EARLY, POLARS):
                polar_step(p)
        for first in range(0, az_rows, 8):
            value = jnp.dot(
                field[f, first * z_rows : (first + 8) * z_rows],
                basis_ref[...],
                preferred_element_type=jnp.float32,
            )
            for i in range(8):
                here = value[i * z_rows : (i + 1) * z_rows]
                there = pl.ds((first + i) * STRIDE, z_rows)
                spectrum[2 * f, there] = here[:, :FREQS]
                spectrum[2 * f + 1, there] = here[:, FREQS:]

    def panel_step(z, carry):
        rows = pl.ds(z, az_rows, stride=STRIDE)
        parts = [spectrum[c, rows] for c in range(4)]
        source = jnp.concatenate(
            [
                jnp.concatenate([parts[0], parts[2]], axis=1),
                jnp.concatenate([parts[1], parts[3]], axis=1),
            ],
            axis=0,
        ).astype(jnp.bfloat16)
        value = jnp.dot(modal, source, preferred_element_type=jnp.float32)
        there = pl.ds(z, ARC_POINTS, stride=STRIDE)
        wave[0, there] = value[:64, :128]
        wave[1, there] = value[64:, :128]
        wave[2, there] = value[:64, 128:]
        wave[3, there] = value[64:, 128:]
        return carry

    lax.fori_loop(0, z_rows, panel_step, 0, unroll=8)

    fetch[5].wait()
    lane = lax.broadcasted_iota(jnp.int32, (8, 128), 1)
    per_block = ids_ref.shape[0] // (az_count * obs_count)
    z_count = az_count // 2
    twist = (obs >> 1) ^ (az // z_count)

    def observer_step(block, carry):
        y = 1 - block // z_count
        z = block % z_count
        z = jnp.where(z < z_count // 2, z + z_count // 2, z_count - 1 - z)
        there_obs = 2 * (twist ^ y) + (obs & 1)
        first_id = ((y * z_count + z) * obs_count + there_obs) * per_block
        for j in range(per_block):
            where = ids_ref[first_id + j]
            p, q = where >> 6, where & 63
            rows = pl.ds(pl.multiple_of(q * STRIDE, 8), z_rows)
            k0, k1, k2, k3 = (green[p, c] for c in range(4))
            w0, w1, w2, w3 = (wave[c, rows] for c in range(4))
            re = (k0 * w0 - k1 * w1) + (k2 * w2 - k3 * w3)
            im = (k0 * w1 + k1 * w0) + (k2 * w3 + k3 * w2)
            there = pl.ds(pl.multiple_of((block * per_block + j) * 8, 8), 8)
            sums[0, there] = jnp.sum(re.reshape(z_rows // 8, 8, 128), axis=0)
            sums[1, there] = jnp.sum(im.reshape(z_rows // 8, 8, 128), axis=0)
        return carry

    lax.fori_loop(0, az_count, observer_step, 0, unroll=4)

    def gather_step(block, carry):
        pieces = []
        for part in range(2):
            halves = []
            for half in range(2):
                first = (block * per_block + half * 8) * 8
                rows = [sums[part, pl.ds(first + i, 8, stride=8)] for i in range(8)]
                while len(rows) > 1:
                    rows = [x + y for x, y in zip(rows[::2], rows[1::2])]
                halves.append(rows[0])
            low, high = halves
            pieces.append(jnp.where(lane < 64, low, pltpu.roll(high, 64, 1)))
            pieces.append(jnp.where(lane < 64, pltpu.roll(low, 64, 1), high))
        rows = pl.ds(pl.multiple_of(block * 32, 32), 32)
        out_ref[rows] = jnp.concatenate([pieces[ax] for ax in AX_ORDER], axis=0).astype(
            jnp.bfloat16
        )
        return carry

    lax.fori_loop(0, az_count, gather_step, 0, unroll=8)


def shards(thickness, loading, kept_modes, cap_stations, observer_ids):
    az_rows, z_rows, samples = thickness.shape
    az_count = lax.axis_size("az")
    ax_count = lax.axis_size("ax")
    obs_count = lax.axis_size("obs")
    total_az = az_rows * az_count
    total_z = z_rows * ax_count
    basis = jnp.asarray(time_table(samples, FREQS))
    flat = (az_rows * z_rows, samples)

    def body(*refs):
        far_field(az_rows, z_rows, az_count, obs_count, total_az, total_z, *refs)

    anywhere = pl.BlockSpec(memory_space=pl.ANY)
    partial_value = pl.pallas_call(
        body,
        out_shape=pltpu.VMEM((az_count * ax_count * 8, 128), jnp.bfloat16),
        in_specs=[anywhere] * 6,
        out_specs=pl.BlockSpec(memory_space=pltpu.VMEM),
        scratch_shapes=[
            pltpu.SMEM(observer_ids.shape, jnp.int32),
            pltpu.SMEM(cap_stations.shape, jnp.int32),
            pltpu.VMEM((1, MODES), jnp.int32),
            pltpu.VMEM(basis.shape, jnp.bfloat16),
            pltpu.VMEM((2, *flat), jnp.bfloat16),
            pltpu.VMEM((4, (az_rows + 1) * STRIDE, FREQS), jnp.float32),
            pltpu.VMEM((4, (ARC_POINTS + 1) * STRIDE, FREQS), jnp.float32),
            pltpu.VMEM((POLARS, 4, z_rows, FREQS), jnp.float32),
            pltpu.VMEM((2, observer_ids.shape[0] // obs_count * 8 + 8, FREQS), jnp.float32),
            pltpu.SemaphoreType.DMA((6,)),
        ],
        compiler_params=pltpu.CompilerParams(vmem_limit_bytes=60 * 1024 * 1024),
        name="far_field",
    )(
        observer_ids,
        cap_stations,
        kept_modes.reshape(1, MODES),
        basis,
        thickness.reshape(flat),
        loading.reshape(flat),
    )
    pieces = partial_value.reshape(az_count * ax_count, 8, 128)
    arrived = lax.all_to_all(
        pieces,
        ("az", "ax", "obs"),
        split_axis=0,
        concat_axis=0,
        axis_index_groups=exchange_groups(az_count, ax_count, obs_count),
        tiled=True,
    )
    total = jnp.sum(arrived.astype(jnp.float32), axis=0)
    return jnp.concatenate([total[:, :64], total[:, 64:]], axis=0)


def solution(mesh):
    return jax.shard_map(
        shards,
        mesh=mesh,
        in_specs=(P("az", "ax", None), P("az", "ax", None), P(), P(), P()),
        out_specs=P(("az", "obs"), "ax"),
        check_vma=False,
    )
```

```python
import math

import jax
import jax.numpy as jnp
import numpy as np
from jax import lax
from jax.experimental import pallas as pl
from jax.experimental.pallas import tpu as pltpu
from jax.sharding import PartitionSpec as P

FREQS = 128
MODES = 64
POLARS = 32
ARC_POINTS = 64
EARLY = 24
STRIDE = 40

SPACING = 0.1
RADIUS = 1.0
ARC = 10.0
KMAX = 6.0


Y_ORDER = (1, 0)
Z_ORDER = (4, 5, 6, 7, 3, 2, 1, 0)
AX_ORDER = (2, 3, 1, 0)


def exchange_groups(az_count, ax_count, obs_count):
    z_count = az_count // 2
    groups = []
    for twist in range(obs_count // 2):
        for core in range(2):
            groups.append(
                [
                    ((y * z_count + z) * ax_count + ax) * obs_count + 2 * (twist ^ y) + core
                    for y in Y_ORDER
                    for z in Z_ORDER
                    for ax in AX_ORDER
                ]
            )
    return groups


def even_odd_series():
    nodes = np.cos((np.arange(64) + 0.5) * np.pi / 64) * 0.5 + 0.5
    root = np.sqrt(nodes)
    fit = np.polynomial.chebyshev.Chebyshev.fit
    even = fit(nodes, np.cos(np.pi * root), 7, domain=[0, 1]).convert(kind=np.polynomial.Polynomial)
    odd = fit(nodes, np.sin(np.pi * root) / root, 6, domain=[0, 1]).convert(
        kind=np.polynomial.Polynomial
    )
    return (
        [float(c) * 4.0**i for i, c in enumerate(even.coef)],
        [2.0 * float(c) * 4.0**i for i, c in enumerate(odd.coef)],
    )


EVEN, ODD = even_odd_series()


def series(coefficients, square):
    total = jnp.full_like(square, coefficients[-1])
    for c in coefficients[-2::-1]:
        total = total * square + c
    return total


def cos_sin_turns(turns):
    part = turns - jnp.round(turns)
    square = part * part
    return series(EVEN, square), part * series(ODD, square)


def time_table(samples, bin_count):
    steps = np.arange(samples)
    bins = np.arange(bin_count) + 1
    angle = 2.0 * np.pi / samples * (steps[:, None] * bins[None, :] % samples)
    window = 0.5 - 0.5 * np.cos(2.0 * np.pi / samples * steps)
    basis = np.concatenate([window[:, None] * np.cos(angle), -window[:, None] * np.sin(angle)], 1)
    return (basis * (2.0 / math.sqrt(samples))).astype(np.float32).astype(jnp.bfloat16)


def far_field(
    az_rows,
    z_rows,
    az_count,
    obs_count,
    total_az,
    total_z,
    ids_from,
    caps_from,
    modes_from,
    basis_from,
    thick_from,
    load_from,
    out_ref,
    ids_ref,
    caps_ref,
    modes_ref,
    basis_ref,
    field,
    spectrum,
    wave,
    green,
    sums,
    sems,
):
    fetch = [
        pltpu.make_async_copy(source, target, sems.at[i])
        for i, (source, target) in enumerate(
            (
                (caps_from, caps_ref),
                (modes_from, modes_ref),
                (basis_from, basis_ref),
                (thick_from, field.at[0]),
                (load_from, field.at[1]),
                (ids_from, ids_ref),
            )
        )
    ]
    for copy in fetch:
        copy.start()
    az, ax, obs = lax.axis_index("az"), lax.axis_index("ax"), lax.axis_index("obs")

    fetch[0].wait()
    bins = (lax.broadcasted_iota(jnp.int32, (1, 128), 1) + 1).astype(jnp.float32)
    wavenumber = KMAX / FREQS * bins
    panel = lax.broadcasted_iota(jnp.int32, (z_rows, 128), 0) + ax * z_rows
    weight = jnp.zeros((z_rows, 128), jnp.float32)
    for c in range(caps_ref.shape[0]):
        weight += (panel < caps_ref[c]).astype(jnp.float32)
    weight *= 1.0 / (caps_ref.shape[0] * math.sqrt(total_z * MODES))
    axial_panel = (panel.astype(jnp.float32) + 0.5) * SPACING

    def polar_step(p):
        index = jnp.full((8, 128), p, jnp.int32).astype(jnp.float32)
        cos_theta, sin_theta = cos_sin_turns((20.0 + index * (140.0 / 31.0)) * (1.0 / 360.0))
        axial = (0.5 * SPACING * total_z + ARC * cos_theta)[:1]
        radial = (ARC * sin_theta)[:1]
        offset = axial - axial_panel
        distance = jnp.sqrt(offset * offset + (radial * radial + RADIUS * RADIUS))
        inverse = 1.0 / distance
        ratio = radial * inverse
        scaled = inverse * weight
        cos_phase, sin_phase = cos_sin_turns(distance * (wavenumber * (0.5 / math.pi)))
        re = cos_phase * scaled
        im = -sin_phase * scaled
        wave_re = wavenumber * re
        wave_im = wavenumber * im
        green[p, 0] = -wave_im
        green[p, 1] = wave_re
        green[p, 2] = ratio * (re * inverse - wave_im)
        green[p, 3] = ratio * (wave_re + im * inverse)

    for p in range(EARLY):
        polar_step(p)

    fetch[1].wait()
    modes = jnp.concatenate([modes_ref[...], modes_ref[...]], axis=1)
    row = lax.broadcasted_iota(jnp.int32, (128, 128), 0)
    column = lax.broadcasted_iota(jnp.int32, (128, 128), 1)
    quarter = 256 * ((row >> 6) + (column >> 6))
    arc_phase = ((row & 63) * modes & 63) * (1024 // ARC_POINTS) - quarter
    arc, _ = cos_sin_turns(arc_phase.astype(jnp.float32) * (1.0 / 1024))
    turn = ((row & 63) + az * az_rows) * modes & (total_az - 1)
    ring, _ = cos_sin_turns((turn * (1024 // total_az) - quarter).astype(jnp.float32) * (1.0 / 1024))
    ring = (ring * (1.0 / math.sqrt(total_az))).astype(jnp.bfloat16)
    arc_high = arc.astype(jnp.bfloat16)
    arc_low = (arc - arc_high.astype(jnp.float32)).astype(jnp.bfloat16)
    contract = (((1,), (1,)), ((), ()))
    modal = lax.dot_general(arc_high, ring, contract, preferred_element_type=jnp.float32)
    modal += lax.dot_general(arc_low, ring, contract, preferred_element_type=jnp.float32)
    modal = modal.astype(jnp.bfloat16)

    pitch, arc_pitch = az_rows * STRIDE, ARC_POINTS * STRIDE
    sum_pitch = ids_ref.shape[0] // obs_count * 8
    fetch[2].wait()
    for f in range(2):
        fetch[3 + f].wait()
        if f == 0:
            for p in range(EARLY, POLARS):
                polar_step(p)
        for first in range(0, az_rows, 8):
            value = jnp.dot(
                field[f, first * z_rows : (first + 8) * z_rows],
                basis_ref[...],
                preferred_element_type=jnp.float32,
            )
            for i in range(8):
                here = value[i * z_rows : (i + 1) * z_rows]
                there = 2 * f * pitch + (first + i) * STRIDE
                spectrum[pl.ds(there, z_rows)] = here[:, :FREQS]
                spectrum[pl.ds(there + pitch, z_rows)] = here[:, FREQS:]

    def panel_step(z, carry):
        parts = [spectrum[pl.ds(c * pitch + z, az_rows, stride=STRIDE)] for c in range(4)]
        source = jnp.concatenate(
            [
                jnp.concatenate([parts[0], parts[2]], axis=1),
                jnp.concatenate([parts[1], parts[3]], axis=1),
            ],
            axis=0,
        ).astype(jnp.bfloat16)
        value = jnp.dot(modal, source, preferred_element_type=jnp.float32)
        quarters = (value[:64, :128], value[64:, :128], value[:64, 128:], value[64:, 128:])
        for c, part in enumerate(quarters):
            wave[pl.ds(c * arc_pitch + z, ARC_POINTS, stride=STRIDE)] = part
        return carry

    lax.fori_loop(0, z_rows, panel_step, 0, unroll=8)

    fetch[5].wait()
    lane = lax.broadcasted_iota(jnp.int32, (8, 128), 1)
    per_block = ids_ref.shape[0] // (az_count * obs_count)
    z_count = az_count // 2
    twist = (obs >> 1) ^ (az // z_count)

    def observer_step(block, carry):
        y = 1 - block // z_count
        z = block % z_count
        z = jnp.where(z < z_count // 2, z + z_count // 2, z_count - 1 - z)
        there_obs = 2 * (twist ^ y) + (obs & 1)
        first_id = ((y * z_count + z) * obs_count + there_obs) * per_block
        for j in range(per_block):
            where = ids_ref[first_id + j]
            p, q = where >> 6, where & 63
            first = pl.multiple_of(q * STRIDE, 8)
            k0, k1, k2, k3 = (green[p, c] for c in range(4))
            w0, w1, w2, w3 = (wave[pl.ds(c * arc_pitch + first, z_rows)] for c in range(4))
            re = (k0 * w0 - k1 * w1) + (k2 * w2 - k3 * w3)
            im = (k0 * w1 + k1 * w0) + (k2 * w3 + k3 * w2)
            there = pl.multiple_of((block * per_block + j) * 8, 8)
            sums[pl.ds(there, 8)] = jnp.sum(re.reshape(z_rows // 8, 8, 128), axis=0)
            sums[pl.ds(sum_pitch + there, 8)] = jnp.sum(im.reshape(z_rows // 8, 8, 128), axis=0)
        return carry

    lax.fori_loop(0, az_count, observer_step, 0, unroll=4)

    def gather_step(block, carry):
        pieces = []
        for part in range(2):
            halves = []
            for half in range(2):
                first = part * sum_pitch + (block * per_block + half * 8) * 8
                rows = [sums[pl.ds(first + i, 8, stride=8)] for i in range(8)]
                while len(rows) > 1:
                    rows = [x + y for x, y in zip(rows[::2], rows[1::2])]
                halves.append(rows[0])
            low, high = halves
            pieces.append(jnp.where(lane < 64, low, pltpu.roll(high, 64, 1)))
            pieces.append(jnp.where(lane < 64, pltpu.roll(low, 64, 1), high))
        rows = pl.ds(pl.multiple_of(block * 32, 32), 32)
        out_ref[rows] = jnp.concatenate([pieces[ax] for ax in AX_ORDER], axis=0).astype(
            jnp.bfloat16
        )
        return carry

    lax.fori_loop(0, az_count, gather_step, 0, unroll=8)


def shards(thickness, loading, kept_modes, cap_stations, observer_ids):
    az_rows, z_rows, samples = thickness.shape
    az_count = lax.axis_size("az")
    ax_count = lax.axis_size("ax")
    obs_count = lax.axis_size("obs")
    total_az = az_rows * az_count
    total_z = z_rows * ax_count
    basis = jnp.asarray(time_table(samples, FREQS))
    flat = (az_rows * z_rows, samples)

    def body(*refs):
        far_field(az_rows, z_rows, az_count, obs_count, total_az, total_z, *refs)

    anywhere = pl.BlockSpec(memory_space=pl.ANY)
    partial_value = pl.pallas_call(
        body,
        out_shape=pltpu.VMEM((az_count * ax_count * 8, 128), jnp.bfloat16),
        in_specs=[anywhere] * 6,
        out_specs=pl.BlockSpec(memory_space=pltpu.VMEM),
        scratch_shapes=[
            pltpu.SMEM(observer_ids.shape, jnp.int32),
            pltpu.SMEM(cap_stations.shape, jnp.int32),
            pltpu.VMEM((1, MODES), jnp.int32),
            pltpu.VMEM(basis.shape, jnp.bfloat16),
            pltpu.VMEM((2, *flat), jnp.bfloat16),
            pltpu.VMEM((4 * az_rows * STRIDE + STRIDE, FREQS), jnp.float32),
            pltpu.VMEM((4 * ARC_POINTS * STRIDE + STRIDE, FREQS), jnp.float32),
            pltpu.VMEM((POLARS, 4, z_rows, FREQS), jnp.float32),
            pltpu.VMEM((2 * observer_ids.shape[0] // obs_count * 8 + 8, FREQS), jnp.float32),
            pltpu.SemaphoreType.DMA((6,)),
        ],
        compiler_params=pltpu.CompilerParams(vmem_limit_bytes=60 * 1024 * 1024),
        name="far_field",
    )(
        observer_ids,
        cap_stations,
        kept_modes.reshape(1, MODES),
        basis,
        thickness.reshape(flat),
        loading.reshape(flat),
    )
    pieces = partial_value.reshape(az_count * ax_count, 8, 128)
    arrived = lax.all_to_all(
        pieces,
        ("az", "ax", "obs"),
        split_axis=0,
        concat_axis=0,
        axis_index_groups=exchange_groups(az_count, ax_count, obs_count),
        tiled=True,
    )
    total = jnp.sum(arrived.astype(jnp.float32), axis=0)
    return jnp.concatenate([total[:, :64], total[:, 64:]], axis=0)


def solution(mesh):
    return jax.shard_map(
        shards,
        mesh=mesh,
        in_specs=(P("az", "ax", None), P("az", "ax", None), P(), P(), P()),
        out_specs=P(("az", "obs"), "ax"),
        check_vma=False,
    )
```

```python
import math

import jax
import jax.numpy as jnp
import numpy as np
from jax import lax
from jax.experimental import pallas as pl
from jax.experimental.pallas import tpu as pltpu
from jax.sharding import PartitionSpec as P

FREQS = 128
MODES = 64
POLARS = 32
ARC_POINTS = 64
EARLY = 24
STRIDE = 40

SPACING = 0.1
RADIUS = 1.0
ARC = 10.0
KMAX = 6.0


Y_ORDER = (1, 0)
Z_ORDER = (4, 5, 6, 7, 3, 2, 1, 0)
AX_ORDER = (2, 3, 1, 0)


def exchange_groups(az_count, ax_count, obs_count):
    z_count = az_count // 2
    groups = []
    for twist in range(obs_count // 2):
        for core in range(2):
            groups.append(
                [
                    ((y * z_count + z) * ax_count + ax) * obs_count + 2 * (twist ^ y) + core
                    for y in Y_ORDER
                    for z in Z_ORDER
                    for ax in AX_ORDER
                ]
            )
    return groups


def even_odd_series():
    nodes = np.cos((np.arange(64) + 0.5) * np.pi / 64) * 0.5 + 0.5
    root = np.sqrt(nodes)
    fit = np.polynomial.chebyshev.Chebyshev.fit
    even = fit(nodes, np.cos(np.pi * root), 7, domain=[0, 1]).convert(kind=np.polynomial.Polynomial)
    odd = fit(nodes, np.sin(np.pi * root) / root, 6, domain=[0, 1]).convert(
        kind=np.polynomial.Polynomial
    )
    return (
        [float(c) * 4.0**i for i, c in enumerate(even.coef)],
        [2.0 * float(c) * 4.0**i for i, c in enumerate(odd.coef)],
    )


EVEN, ODD = even_odd_series()


def series(coefficients, square):
    total = jnp.full_like(square, coefficients[-1])
    for c in coefficients[-2::-1]:
        total = total * square + c
    return total


def cos_sin_turns(turns):
    part = turns - jnp.round(turns)
    square = part * part
    return series(EVEN, square), part * series(ODD, square)


def time_table(samples, bin_count):
    steps = np.arange(samples)
    bins = np.arange(bin_count) + 1
    angle = 2.0 * np.pi / samples * (steps[:, None] * bins[None, :] % samples)
    window = 0.5 - 0.5 * np.cos(2.0 * np.pi / samples * steps)
    basis = np.concatenate([window[:, None] * np.cos(angle), -window[:, None] * np.sin(angle)], 1)
    return (basis * (2.0 / math.sqrt(samples))).astype(np.float32).astype(jnp.bfloat16)


def far_field(
    az_rows,
    z_rows,
    az_count,
    obs_count,
    total_az,
    total_z,
    ids_from,
    caps_from,
    modes_from,
    basis_from,
    thick_from,
    load_from,
    out_ref,
    ids_ref,
    caps_ref,
    modes_ref,
    basis_ref,
    field,
    spectrum0,
    spectrum1,
    wave0,
    wave1,
    green,
    sums0,
    sums1,
    sems,
):
    spectrum, wave, sums = (spectrum0, spectrum1), (wave0, wave1), (sums0, sums1)
    fetch = [
        pltpu.make_async_copy(source, target, sems.at[i])
        for i, (source, target) in enumerate(
            (
                (caps_from, caps_ref),
                (modes_from, modes_ref),
                (basis_from, basis_ref),
                (thick_from, field.at[0]),
                (load_from, field.at[1]),
                (ids_from, ids_ref),
            )
        )
    ]
    for copy in fetch:
        copy.start()
    az, ax, obs = lax.axis_index("az"), lax.axis_index("ax"), lax.axis_index("obs")

    fetch[0].wait()
    bins = (lax.broadcasted_iota(jnp.int32, (1, 128), 1) + 1).astype(jnp.float32)
    wavenumber = KMAX / FREQS * bins
    panel = lax.broadcasted_iota(jnp.int32, (z_rows, 128), 0) + ax * z_rows
    weight = jnp.zeros((z_rows, 128), jnp.float32)
    for c in range(caps_ref.shape[0]):
        weight += (panel < caps_ref[c]).astype(jnp.float32)
    weight *= 1.0 / (caps_ref.shape[0] * math.sqrt(total_z * MODES))
    axial_panel = (panel.astype(jnp.float32) + 0.5) * SPACING

    def polar_step(p):
        index = jnp.full((8, 128), p, jnp.int32).astype(jnp.float32)
        cos_theta, sin_theta = cos_sin_turns((20.0 + index * (140.0 / 31.0)) * (1.0 / 360.0))
        axial = (0.5 * SPACING * total_z + ARC * cos_theta)[:1]
        radial = (ARC * sin_theta)[:1]
        offset = axial - axial_panel
        distance = jnp.sqrt(offset * offset + (radial * radial + RADIUS * RADIUS))
        inverse = 1.0 / distance
        ratio = radial * inverse
        scaled = inverse * weight
        cos_phase, sin_phase = cos_sin_turns(distance * (wavenumber * (0.5 / math.pi)))
        re = cos_phase * scaled
        im = -sin_phase * scaled
        wave_re = wavenumber * re
        wave_im = wavenumber * im
        green[p, 0] = -wave_im
        green[p, 1] = wave_re
        green[p, 2] = ratio * (re * inverse - wave_im)
        green[p, 3] = ratio * (wave_re + im * inverse)

    for p in range(EARLY):
        polar_step(p)

    fetch[1].wait()
    modes = jnp.concatenate([modes_ref[...], modes_ref[...]], axis=1)
    row = lax.broadcasted_iota(jnp.int32, (128, 128), 0)
    column = lax.broadcasted_iota(jnp.int32, (128, 128), 1)
    quarter = 256 * ((row >> 6) + (column >> 6))
    arc_phase = ((row & 63) * modes & 63) * (1024 // ARC_POINTS) - quarter
    arc, _ = cos_sin_turns(arc_phase.astype(jnp.float32) * (1.0 / 1024))
    turn = ((row & 63) + az * az_rows) * modes & (total_az - 1)
    ring, _ = cos_sin_turns((turn * (1024 // total_az) - quarter).astype(jnp.float32) * (1.0 / 1024))
    ring = (ring * (1.0 / math.sqrt(total_az))).astype(jnp.bfloat16)
    arc_high = arc.astype(jnp.bfloat16)
    arc_low = (arc - arc_high.astype(jnp.float32)).astype(jnp.bfloat16)
    contract = (((1,), (1,)), ((), ()))
    modal = lax.dot_general(arc_high, ring, contract, preferred_element_type=jnp.float32)
    modal += lax.dot_general(arc_low, ring, contract, preferred_element_type=jnp.float32)
    modal = modal.astype(jnp.bfloat16)

    lane = lax.broadcasted_iota(jnp.int32, (8, 128), 1)
    per_block = ids_ref.shape[0] // (az_count * obs_count)
    z_count = az_count // 2
    twist = (obs >> 1) ^ (az // z_count)

    def time_chunk(f, first):
        value = jnp.dot(
            field[f, first * z_rows : (first + 8) * z_rows],
            basis_ref[...],
            preferred_element_type=jnp.float32,
        )
        for i in range(8):
            here = value[i * z_rows : (i + 1) * z_rows]
            there = pl.ds((first + i) * STRIDE, z_rows)
            spectrum[f][0, there] = here[:, :FREQS]
            spectrum[f][1, there] = here[:, FREQS:]

    def panel_pairs(f):
        def pair_step(i, carry):
            parts = [
                [spectrum[f][c, pl.ds(2 * i + k, az_rows, stride=STRIDE)] for k in range(2)]
                for c in range(2)
            ]
            source = jnp.concatenate(
                [jnp.concatenate(part, axis=1) for part in parts], axis=0
            ).astype(jnp.bfloat16)
            value = jnp.dot(modal, source, preferred_element_type=jnp.float32)
            for k in range(2):
                there = pl.ds(2 * i + k, ARC_POINTS, stride=STRIDE)
                columns = value[:, k * FREQS : (k + 1) * FREQS]
                wave[f][0, there] = columns[:64]
                wave[f][1, there] = columns[64:]
            return carry

        lax.fori_loop(0, z_rows // 2, pair_step, 0, unroll=8)

    def observers(f, block):
        y = 1 - block // z_count
        z = block % z_count
        z = jnp.where(z < z_count // 2, z + z_count // 2, z_count - 1 - z)
        there_obs = 2 * (twist ^ y) + (obs & 1)
        first_id = ((y * z_count + z) * obs_count + there_obs) * per_block
        for j in range(per_block):
            where = ids_ref[first_id + j]
            p, q = where >> 6, where & 63
            rows = pl.ds(pl.multiple_of(q * STRIDE, 8), z_rows)
            k0, k1 = green[p, 2 * f], green[p, 2 * f + 1]
            w0, w1 = wave[f][0, rows], wave[f][1, rows]
            re = k0 * w0 - k1 * w1
            im = k0 * w1 + k1 * w0
            there = pl.ds(pl.multiple_of((block * per_block + j) * 8, 8), 8)
            sums[f][0, there] = jnp.sum(re.reshape(z_rows // 8, 8, 128), axis=0)
            sums[f][1, there] = jnp.sum(im.reshape(z_rows // 8, 8, 128), axis=0)

    fetch[2].wait()
    fetch[3].wait()
    for p in range(EARLY, POLARS):
        polar_step(p)
    for first in range(0, az_rows, 8):
        time_chunk(0, first)
    panel_pairs(0)
    fetch[4].wait()
    fetch[5].wait()
    for first in range(0, az_rows, 8):
        time_chunk(1, first)
        observers(0, first // 4)
        observers(0, first // 4 + 1)
    panel_pairs(1)

    def observer_step(block, carry):
        observers(1, block)
        return carry

    lax.fori_loop(0, az_count, observer_step, 0, unroll=4)

    def gather_step(block, carry):
        pieces = []
        for part in range(2):
            halves = []
            for half in range(2):
                first = (block * per_block + half * 8) * 8
                rows = [sums[f][part, pl.ds(first + i, 8, stride=8)] for f in range(2) for i in range(8)]
                while len(rows) > 1:
                    rows = [x + y for x, y in zip(rows[::2], rows[1::2])]
                halves.append(rows[0])
            low, high = halves
            pieces.append(jnp.where(lane < 64, low, pltpu.roll(high, 64, 1)))
            pieces.append(jnp.where(lane < 64, pltpu.roll(low, 64, 1), high))
        rows = pl.ds(pl.multiple_of(block * 32, 32), 32)
        out_ref[rows] = jnp.concatenate([pieces[ax] for ax in AX_ORDER], axis=0).astype(
            jnp.bfloat16
        )
        return carry

    lax.fori_loop(0, az_count, gather_step, 0, unroll=8)


def shards(thickness, loading, kept_modes, cap_stations, observer_ids):
    az_rows, z_rows, samples = thickness.shape
    az_count = lax.axis_size("az")
    ax_count = lax.axis_size("ax")
    obs_count = lax.axis_size("obs")
    total_az = az_rows * az_count
    total_z = z_rows * ax_count
    basis = jnp.asarray(time_table(samples, FREQS))
    flat = (az_rows * z_rows, samples)

    def body(*refs):
        far_field(az_rows, z_rows, az_count, obs_count, total_az, total_z, *refs)

    anywhere = pl.BlockSpec(memory_space=pl.ANY)
    partial_value = pl.pallas_call(
        body,
        out_shape=pltpu.VMEM((az_count * ax_count * 8, 128), jnp.bfloat16),
        in_specs=[anywhere] * 6,
        out_specs=pl.BlockSpec(memory_space=pltpu.VMEM),
        scratch_shapes=[
            pltpu.SMEM(observer_ids.shape, jnp.int32),
            pltpu.SMEM(cap_stations.shape, jnp.int32),
            pltpu.VMEM((1, MODES), jnp.int32),
            pltpu.VMEM(basis.shape, jnp.bfloat16),
            pltpu.VMEM((2, *flat), jnp.bfloat16),
            pltpu.VMEM((2, (az_rows + 1) * STRIDE, FREQS), jnp.float32),
            pltpu.VMEM((2, (az_rows + 1) * STRIDE, FREQS), jnp.float32),
            pltpu.VMEM((2, (ARC_POINTS + 1) * STRIDE, FREQS), jnp.float32),
            pltpu.VMEM((2, (ARC_POINTS + 1) * STRIDE, FREQS), jnp.float32),
            pltpu.VMEM((POLARS, 4, z_rows, FREQS), jnp.float32),
            pltpu.VMEM((2, observer_ids.shape[0] // obs_count * 8 + 8, FREQS), jnp.float32),
            pltpu.VMEM((2, observer_ids.shape[0] // obs_count * 8 + 8, FREQS), jnp.float32),
            pltpu.SemaphoreType.DMA((6,)),
        ],
        compiler_params=pltpu.CompilerParams(vmem_limit_bytes=60 * 1024 * 1024),
        name="far_field",
    )(
        observer_ids,
        cap_stations,
        kept_modes.reshape(1, MODES),
        basis,
        thickness.reshape(flat),
        loading.reshape(flat),
    )
    pieces = partial_value.reshape(az_count * ax_count, 8, 128)
    arrived = lax.all_to_all(
        pieces,
        ("az", "ax", "obs"),
        split_axis=0,
        concat_axis=0,
        axis_index_groups=exchange_groups(az_count, ax_count, obs_count),
        tiled=True,
    )
    total = jnp.sum(arrived.astype(jnp.float32), axis=0)
    return jnp.concatenate([total[:, :64], total[:, 64:]], axis=0)


def solution(mesh):
    return jax.shard_map(
        shards,
        mesh=mesh,
        in_specs=(P("az", "ax", None), P("az", "ax", None), P(), P(), P()),
        out_specs=P(("az", "obs"), "ax"),
        check_vma=False,
    )
```

```python
import math

import jax
import jax.numpy as jnp
import numpy as np
from jax import lax
from jax.experimental import pallas as pl
from jax.experimental.pallas import tpu as pltpu
from jax.sharding import PartitionSpec as P

FREQS = 128
MODES = 64
POLARS = 32
ARC_POINTS = 64
EARLY = 24
STRIDE = 56

SPACING = 0.1
RADIUS = 1.0
ARC = 10.0
KMAX = 6.0


Y_ORDER = (1, 0)
Z_ORDER = (4, 5, 6, 7, 3, 2, 1, 0)
AX_ORDER = (2, 3, 1, 0)


def exchange_groups(az_count, ax_count, obs_count):
    z_count = az_count // 2
    groups = []
    for twist in range(obs_count // 2):
        for core in range(2):
            groups.append(
                [
                    ((y * z_count + z) * ax_count + ax) * obs_count + 2 * (twist ^ y) + core
                    for y in Y_ORDER
                    for z in Z_ORDER
                    for ax in AX_ORDER
                ]
            )
    return groups


def even_odd_series():
    nodes = np.cos((np.arange(64) + 0.5) * np.pi / 64) * 0.5 + 0.5
    root = np.sqrt(nodes)
    fit = np.polynomial.chebyshev.Chebyshev.fit
    even = fit(nodes, np.cos(np.pi * root), 7, domain=[0, 1]).convert(kind=np.polynomial.Polynomial)
    odd = fit(nodes, np.sin(np.pi * root) / root, 6, domain=[0, 1]).convert(
        kind=np.polynomial.Polynomial
    )
    return (
        [float(c) * 4.0**i for i, c in enumerate(even.coef)],
        [2.0 * float(c) * 4.0**i for i, c in enumerate(odd.coef)],
    )


EVEN, ODD = even_odd_series()


def series(coefficients, square):
    total = jnp.full_like(square, coefficients[-1])
    for c in coefficients[-2::-1]:
        total = total * square + c
    return total


def cos_sin_turns(turns):
    part = turns - jnp.round(turns)
    square = part * part
    return series(EVEN, square), part * series(ODD, square)


def time_table(samples, bin_count):
    steps = np.arange(samples)
    bins = np.arange(bin_count) + 1
    angle = 2.0 * np.pi / samples * (steps[:, None] * bins[None, :] % samples)
    window = 0.5 - 0.5 * np.cos(2.0 * np.pi / samples * steps)
    basis = np.concatenate([window[:, None] * np.cos(angle), -window[:, None] * np.sin(angle)], 1)
    return (basis * (2.0 / math.sqrt(samples))).astype(np.float32).astype(jnp.bfloat16)


def far_field(
    az_rows,
    z_rows,
    az_count,
    obs_count,
    total_az,
    total_z,
    ids_from,
    caps_from,
    modes_from,
    basis_from,
    thick_from,
    load_from,
    out_ref,
    ids_ref,
    caps_ref,
    modes_ref,
    basis_ref,
    field,
    spectrum0,
    spectrum1,
    wave0,
    wave1,
    green,
    sums0,
    sums1,
    sems,
):
    spectrum, wave, sums = (spectrum0, spectrum1), (wave0, wave1), (sums0, sums1)
    fetch = [
        pltpu.make_async_copy(source, target, sems.at[i])
        for i, (source, target) in enumerate(
            (
                (caps_from, caps_ref),
                (modes_from, modes_ref),
                (basis_from, basis_ref),
                (thick_from, field.at[0]),
                (load_from, field.at[1]),
                (ids_from, ids_ref),
            )
        )
    ]
    for copy in fetch:
        copy.start()
    az, ax, obs = lax.axis_index("az"), lax.axis_index("ax"), lax.axis_index("obs")

    fetch[0].wait()
    bins = (lax.broadcasted_iota(jnp.int32, (1, 128), 1) + 1).astype(jnp.float32)
    wavenumber = KMAX / FREQS * bins
    panel = lax.broadcasted_iota(jnp.int32, (z_rows, 128), 0) + ax * z_rows
    weight = jnp.zeros((z_rows, 128), jnp.float32)
    for c in range(caps_ref.shape[0]):
        weight += (panel < caps_ref[c]).astype(jnp.float32)
    weight *= 1.0 / (caps_ref.shape[0] * math.sqrt(total_z * MODES))
    axial_panel = (panel.astype(jnp.float32) + 0.5) * SPACING

    def polar_step(p):
        index = jnp.full((8, 128), p, jnp.int32).astype(jnp.float32)
        cos_theta, sin_theta = cos_sin_turns((20.0 + index * (140.0 / 31.0)) * (1.0 / 360.0))
        axial = (0.5 * SPACING * total_z + ARC * cos_theta)[:1]
        radial = (ARC * sin_theta)[:1]
        offset = axial - axial_panel
        distance = jnp.sqrt(offset * offset + (radial * radial + RADIUS * RADIUS))
        inverse = 1.0 / distance
        ratio = radial * inverse
        scaled = inverse * weight
        cos_phase, sin_phase = cos_sin_turns(distance * (wavenumber * (0.5 / math.pi)))
        re = cos_phase * scaled
        im = -sin_phase * scaled
        wave_re = wavenumber * re
        wave_im = wavenumber * im
        green[p, 0] = -wave_im
        green[p, 1] = wave_re
        green[p, 2] = ratio * (re * inverse - wave_im)
        green[p, 3] = ratio * (wave_re + im * inverse)

    for p in range(EARLY):
        polar_step(p)

    fetch[1].wait()
    modes = jnp.concatenate([modes_ref[...], modes_ref[...]], axis=1)
    row = lax.broadcasted_iota(jnp.int32, (128, 128), 0)
    column = lax.broadcasted_iota(jnp.int32, (128, 128), 1)
    quarter = 256 * ((row >> 6) + (column >> 6))
    arc_phase = ((row & 63) * modes & 63) * (1024 // ARC_POINTS) - quarter
    arc, _ = cos_sin_turns(arc_phase.astype(jnp.float32) * (1.0 / 1024))
    turn = ((row & 63) + az * az_rows) * modes & (total_az - 1)
    ring, _ = cos_sin_turns((turn * (1024 // total_az) - quarter).astype(jnp.float32) * (1.0 / 1024))
    ring = (ring * (1.0 / math.sqrt(total_az))).astype(jnp.bfloat16)
    arc_high = arc.astype(jnp.bfloat16)
    arc_low = (arc - arc_high.astype(jnp.float32)).astype(jnp.bfloat16)
    contract = (((1,), (1,)), ((), ()))
    modal = lax.dot_general(arc_high, ring, contract, preferred_element_type=jnp.float32)
    modal += lax.dot_general(arc_low, ring, contract, preferred_element_type=jnp.float32)
    modal = modal.astype(jnp.bfloat16)

    lane = lax.broadcasted_iota(jnp.int32, (8, 128), 1)
    per_block = ids_ref.shape[0] // (az_count * obs_count)
    z_count = az_count // 2
    twist = (obs >> 1) ^ (az // z_count)

    def time_chunk(f, first):
        value = jnp.dot(
            field[f, first * z_rows : (first + 8) * z_rows],
            basis_ref[...],
            preferred_element_type=jnp.float32,
        )
        for i in range(8):
            here = value[i * z_rows : (i + 1) * z_rows]
            there = pl.ds((first + i) * STRIDE, z_rows)
            spectrum[f][0, there] = here[:, :FREQS]
            spectrum[f][1, there] = here[:, FREQS:]

    def panel_pairs(f):
        def pair_step(i, carry):
            parts = [
                [spectrum[f][c, pl.ds(2 * i + k, az_rows, stride=STRIDE)] for k in range(2)]
                for c in range(2)
            ]
            source = jnp.concatenate(
                [jnp.concatenate(part, axis=1) for part in parts], axis=0
            ).astype(jnp.bfloat16)
            value = jnp.dot(modal, source, preferred_element_type=jnp.float32)
            for k in range(2):
                there = pl.ds(2 * i + k, ARC_POINTS, stride=STRIDE)
                columns = value[:, k * FREQS : (k + 1) * FREQS]
                wave[f][0, there] = columns[:64]
                wave[f][1, there] = columns[64:]
            return carry

        lax.fori_loop(0, z_rows // 2, pair_step, 0, unroll=8)

    def observers(f, block):
        y = 1 - block // z_count
        z = block % z_count
        z = jnp.where(z < z_count // 2, z + z_count // 2, z_count - 1 - z)
        there_obs = 2 * (twist ^ y) + (obs & 1)
        first_id = ((y * z_count + z) * obs_count + there_obs) * per_block
        for j in range(per_block):
            where = ids_ref[first_id + j]
            p, q = where >> 6, where & 63
            rows = pl.ds(pl.multiple_of(q * STRIDE, 8), z_rows)
            k0, k1 = green[p, 2 * f], green[p, 2 * f + 1]
            w0, w1 = wave[f][0, rows], wave[f][1, rows]
            re = k0 * w0 - k1 * w1
            im = k0 * w1 + k1 * w0
            there = pl.ds(pl.multiple_of((block * per_block + j) * 8, 8), 8)
            sums[f][0, there] = jnp.sum(re.reshape(z_rows // 8, 8, 128), axis=0)
            sums[f][1, there] = jnp.sum(im.reshape(z_rows // 8, 8, 128), axis=0)

    fetch[2].wait()
    fetch[3].wait()
    for p in range(EARLY, POLARS):
        polar_step(p)
    for first in range(0, az_rows, 8):
        time_chunk(0, first)
    panel_pairs(0)
    fetch[4].wait()
    fetch[5].wait()
    for first in range(0, az_rows, 8):
        time_chunk(1, first)
        observers(0, first // 4)
        observers(0, first // 4 + 1)
    panel_pairs(1)

    def observer_step(block, carry):
        observers(1, block)
        return carry

    lax.fori_loop(0, az_count, observer_step, 0, unroll=4)

    def gather_step(block, carry):
        pieces = []
        for part in range(2):
            halves = []
            for half in range(2):
                first = (block * per_block + half * 8) * 8
                rows = [sums[f][part, pl.ds(first + i, 8, stride=8)] for f in range(2) for i in range(8)]
                while len(rows) > 1:
                    rows = [x + y for x, y in zip(rows[::2], rows[1::2])]
                halves.append(rows[0])
            low, high = halves
            pieces.append(jnp.where(lane < 64, low, pltpu.roll(high, 64, 1)))
            pieces.append(jnp.where(lane < 64, pltpu.roll(low, 64, 1), high))
        rows = pl.ds(pl.multiple_of(block * 32, 32), 32)
        out_ref[rows] = jnp.concatenate([pieces[ax] for ax in AX_ORDER], axis=0).astype(
            jnp.bfloat16
        )
        return carry

    lax.fori_loop(0, az_count, gather_step, 0, unroll=8)


def shards(thickness, loading, kept_modes, cap_stations, observer_ids):
    az_rows, z_rows, samples = thickness.shape
    az_count = lax.axis_size("az")
    ax_count = lax.axis_size("ax")
    obs_count = lax.axis_size("obs")
    total_az = az_rows * az_count
    total_z = z_rows * ax_count
    basis = jnp.asarray(time_table(samples, FREQS))
    flat = (az_rows * z_rows, samples)

    def body(*refs):
        far_field(az_rows, z_rows, az_count, obs_count, total_az, total_z, *refs)

    anywhere = pl.BlockSpec(memory_space=pl.ANY)
    partial_value = pl.pallas_call(
        body,
        out_shape=pltpu.VMEM((az_count * ax_count * 8, 128), jnp.bfloat16),
        in_specs=[anywhere] * 6,
        out_specs=pl.BlockSpec(memory_space=pltpu.VMEM),
        scratch_shapes=[
            pltpu.SMEM(observer_ids.shape, jnp.int32),
            pltpu.SMEM(cap_stations.shape, jnp.int32),
            pltpu.VMEM((1, MODES), jnp.int32),
            pltpu.VMEM(basis.shape, jnp.bfloat16),
            pltpu.VMEM((2, *flat), jnp.bfloat16),
            pltpu.VMEM((2, (az_rows + 1) * STRIDE, FREQS), jnp.float32),
            pltpu.VMEM((2, (az_rows + 1) * STRIDE, FREQS), jnp.float32),
            pltpu.VMEM((2, (ARC_POINTS + 1) * STRIDE, FREQS), jnp.float32),
            pltpu.VMEM((2, (ARC_POINTS + 1) * STRIDE, FREQS), jnp.float32),
            pltpu.VMEM((POLARS, 4, z_rows, FREQS), jnp.float32),
            pltpu.VMEM((2, observer_ids.shape[0] // obs_count * 8 + 8, FREQS), jnp.float32),
            pltpu.VMEM((2, observer_ids.shape[0] // obs_count * 8 + 8, FREQS), jnp.float32),
            pltpu.SemaphoreType.DMA((6,)),
        ],
        compiler_params=pltpu.CompilerParams(vmem_limit_bytes=60 * 1024 * 1024),
        name="far_field",
    )(
        observer_ids,
        cap_stations,
        kept_modes.reshape(1, MODES),
        basis,
        thickness.reshape(flat),
        loading.reshape(flat),
    )
    pieces = partial_value.reshape(az_count * ax_count, 8, 128)
    arrived = lax.all_to_all(
        pieces,
        ("az", "ax", "obs"),
        split_axis=0,
        concat_axis=0,
        axis_index_groups=exchange_groups(az_count, ax_count, obs_count),
        tiled=True,
    )
    total = jnp.sum(arrived.astype(jnp.float32), axis=0)
    return jnp.concatenate([total[:, :64], total[:, 64:]], axis=0)


def solution(mesh):
    return jax.shard_map(
        shards,
        mesh=mesh,
        in_specs=(P("az", "ax", None), P("az", "ax", None), P(), P(), P()),
        out_specs=P(("az", "obs"), "ax"),
        check_vma=False,
    )
```
